32 devices in a mesh: ctx: 8 (over z, y), tp: 4 (over x, core).
Axes of the slice: x: 2, y: 2, z: 4, core: 2. Of those that a mesh axis runs over, the one named last changes fastest.
Arguments:
- tokens: bfloat16 [2048, 2048], P('ctx'), may hold values from -6 to 6
- w_query: bfloat16 [2048, 4096], P(None, 'tp'), may hold values from -0.125 to 0.125
- w_key: bfloat16 [2048, 512], replicated, may hold values from -0.125 to 0.125
- w_value: bfloat16 [2048, 512], replicated, may hold values from -0.125 to 0.125
- w_out: bfloat16 [4096, 2048], P('tp'), may hold values from -0.09375 to 0.09375
- query_gain: float32 [128], replicated, may hold values from 0.5 to 2
- key_gain: float32 [128], replicated, may hold values from 0.5 to 2
- doc_lengths: int32 [16], replicated, may hold values from 1 to 1024, as said below
Outputs:
- layer_out: bfloat16 [2048, 2048], P('ctx', 'tp')
The draws below stay inside these ranges and needn't reach their ends.
Inputs may be any that keep to these rules, and one draw needn't show every extreme that they name: `doc_lengths`: the lengths sum to 2048; the second-to-last document has exactly 1024 tokens and the last one exactly 128.
All inputs are finite; a program needn't handle non-finite values.
Results may differ from the reference program's by a relative error of at most 0.014.
Values may be sent and summed in bfloat16 or wider, within the bound.
A program may use at most 64 MiB of HBM per device.

```python
import math
import jax
import jax.numpy as jnp
from jax import lax

D = 2048
H = 32
KVH = 4
HD = 128
TOK_DEV = 256
TOKENS = 2048
REACH = 4
MAXDOC = 1024
DOCS = 16
N_TP = 4


def draw_doc_lengths(key, part):
    rest_count = DOCS - 2
    tail_doc = TOK_DEV // 2
    spare = TOKENS - MAXDOC - tail_doc - rest_count
    long_count = max(2, DOCS // 32)
    long_budget = spare * 3 // 4
    order = jax.random.permutation(jax.random.fold_in(key, 23), rest_count).astype(jnp.int32)
    chosen = order[:long_count]
    is_long = jnp.zeros((rest_count,), jnp.int32).at[chosen].set(1)
    long_pick = MAXDOC // 4 + jax.random.randint(jax.random.fold_in(key, 29), (rest_count,), 0, MAXDOC - MAXDOC // 4).astype(jnp.int32)
    long_draw = (long_pick * is_long).astype(jnp.int32)
    long_total = jnp.sum(long_draw).astype(jnp.int32)
    scaled = jnp.where(long_total > long_budget, long_draw * long_budget // jnp.maximum(long_total, 1), long_draw).astype(jnp.int32)
    remaining = (spare - jnp.sum(scaled)).astype(jnp.int32)
    short_mask = (1 - is_long).astype(jnp.int32)
    weights = (jax.random.randint(jax.random.fold_in(key, 17), (rest_count,), 1, 9).astype(jnp.int32) * short_mask).astype(jnp.int32)
    short_extra = (remaining * weights // jnp.sum(weights)).astype(jnp.int32)
    leftover = (remaining - jnp.sum(short_extra)).astype(jnp.int32)
    short_rank = (jnp.cumsum(short_mask) - 1).astype(jnp.int32)
    bump = (short_mask * (short_rank < leftover).astype(jnp.int32)).astype(jnp.int32)
    extra = (scaled + short_extra + bump).astype(jnp.int32)
    long_doc = jnp.full((1,), MAXDOC, jnp.int32)
    last_doc = jnp.full((1,), tail_doc, jnp.int32)
    return jnp.concatenate([(1 + extra).astype(jnp.int32), long_doc, last_doc])


def steps_of(own_key, extent, pieces, smallest, top_value):
    def one(position, parts):
        steps = jax.random.uniform(jax.random.fold_in(jax.random.fold_in(own_key, 6), position), (parts,), jnp.float32, smallest / len(pieces), top_value / len(pieces))
        return jnp.repeat(jnp.exp(steps), extent[position] // parts).reshape((-1,) + (1,) * (len(extent) - position - 1))

    loudness = one(*pieces[0])
    for cut in pieces[1:]:
        loudness = loudness * one(*cut)
    return loudness


def noise(rng, shape, scale, bound, pieces=(), kind=jnp.bfloat16):
    values = jax.random.normal(rng, shape, jnp.float32) * scale
    if len(pieces) > 0:
        values = steps_of(rng, shape, pieces, -0.22, 0.18) * values
    return jnp.clip(values, min=-bound, max=bound).astype(kind)


def setup_inputs(seed: int = 0) -> dict:
    key_of = jax.random.split(jax.random.key(seed), 9)
    tokens = noise(key_of[0], (TOKENS, D), 1.0, 6.0, ((0, 8),))
    w_query = noise(key_of[1], (D, H * HD), D ** -0.5, 0.125, ((1, 4),))
    w_key = noise(key_of[2], (D, KVH * HD), D ** -0.5, 0.125)
    w_value = noise(key_of[3], (D, KVH * HD), D ** -0.5, 0.125)
    w_out = noise(key_of[4], (H * HD, D), (H * HD) ** -0.5, 0.09375, ((0, 4),))
    query_gain = jnp.clip(jnp.exp(jax.random.uniform(key_of[5], (HD,), jnp.float32, math.log(0.5), math.log(2.0))), 0.5, 2.0)
    key_gain = jnp.clip(jnp.exp(jax.random.uniform(key_of[6], (HD,), jnp.float32, math.log(0.5), math.log(2.0))), 0.5, 2.0)
    doc_lengths = draw_doc_lengths(jax.random.fold_in(key_of[8], 71), 0)
    return {"tokens": tokens, "w_query": w_query, "w_key": w_key, "w_value": w_value, "w_out": w_out, "query_gain": query_gain, "key_gain": key_gain, "doc_lengths": doc_lengths}


EPSILON = 1e-06
ROPE_BASE = 1000000.0
NEGATIVE = -1e+30

def doc_starts(positions, doc_lengths):
    doc_ends = jnp.cumsum(doc_lengths).astype(jnp.int32)
    before = doc_ends[None, :] <= positions[:, None]
    return lax.optimization_barrier(jnp.sum(jnp.where(before, doc_lengths[None, :], 0), axis=1)).astype(jnp.int32)

def norm_rotate(inputs, gain_vec, offsets):
    full_width = inputs.shape[-1]
    half_width = full_width // 2
    inv_norm = lax.rsqrt(lax.optimization_barrier(jnp.mean(inputs * inputs, axis=-1, keepdims=True)) + EPSILON)
    normed = inputs * inv_norm * gain_vec
    frequency = ROPE_BASE ** (-2.0 * jnp.arange(half_width, dtype=jnp.float32) / full_width)
    angles = offsets[:, None] * frequency[None, :]
    cosine = jnp.cos(angles)[:, None, :]
    sine_part = jnp.sin(angles)[:, None, :]
    first_half = normed[..., :half_width]
    second_half = normed[..., half_width:]
    return jnp.concatenate([first_half * cosine - second_half * sine_part, second_half * cosine + first_half * sine_part], axis=-1)

def reference(tokens, w_query, w_key, w_value, w_out, query_gain, key_gain, doc_lengths):
    positions = jnp.arange(TOKENS, dtype=jnp.int32)
    starts_all = doc_starts(positions, doc_lengths)
    offsets = (positions - starts_all).astype(jnp.float32)
    queries = norm_rotate(jnp.dot(tokens, w_query, preferred_element_type=jnp.float32).reshape(TOKENS, H, HD), query_gain, offsets).astype(jnp.bfloat16)
    keys_all = norm_rotate(jnp.dot(tokens, w_key, preferred_element_type=jnp.float32).reshape(TOKENS, KVH, HD), key_gain, offsets).astype(jnp.bfloat16)
    values_all = jnp.dot(tokens, w_value, preferred_element_type=jnp.float32).astype(jnp.bfloat16).reshape(TOKENS, KVH, HD)
    key_span = REACH * TOK_DEV
    padding = jnp.zeros((key_span, KVH, HD), jnp.bfloat16)
    keys_padded = jnp.concatenate([padding, keys_all], axis=0)
    values_padded = jnp.concatenate([padding, values_all], axis=0)
    group_size = H // KVH

    def attend_block(block_index):
        start_row = (block_index * TOK_DEV).astype(jnp.int32)
        query_block = lax.dynamic_slice_in_dim(queries, start_row, TOK_DEV, 0).astype(jnp.float32).reshape(TOK_DEV, KVH, group_size, HD)
        key_block = lax.dynamic_slice_in_dim(keys_padded, start_row, key_span + TOK_DEV, 0).astype(jnp.float32)
        value_block = lax.dynamic_slice_in_dim(values_padded, start_row, key_span + TOK_DEV, 0).astype(jnp.float32)
        query_pos = start_row + jnp.arange(TOK_DEV, dtype=jnp.int32)
        query_start = lax.dynamic_slice_in_dim(starts_all, start_row, TOK_DEV, 0)
        key_pos = start_row - key_span + jnp.arange(key_span + TOK_DEV, dtype=jnp.int32)
        visible = (key_pos[None, :] <= query_pos[:, None]) & (key_pos[None, :] >= query_start[:, None])
        scores = jnp.einsum('tgjd,sgd->gjts', query_block, key_block) * HD ** (-0.5)
        row_peak = lax.optimization_barrier(jnp.max(jnp.where(visible, scores, NEGATIVE), axis=-1, keepdims=True))
        weights = jnp.where(visible, jnp.exp(scores - row_peak), 0.0)
        row_total = lax.optimization_barrier(jnp.sum(weights, axis=-1))
        rounded = lax.optimization_barrier(weights.astype(jnp.bfloat16)).astype(jnp.float32)
        mixed = jnp.einsum('gjts,sgd->tgjd', rounded, value_block)
        mixed = mixed / jnp.transpose(row_total, (2, 0, 1))[..., None]
        return mixed.reshape(TOK_DEV, H * HD).astype(jnp.bfloat16)
    attended = lax.map(attend_block, jnp.arange(TOKENS // TOK_DEV, dtype=jnp.int32)).reshape(TOKENS, H * HD)
    group_cols = H // N_TP * HD
    summed = jnp.zeros((TOKENS, D), jnp.float32)
    for tp_rank in range(N_TP):
        head_term = jnp.dot(attended[:, tp_rank * group_cols:(tp_rank + 1) * group_cols], w_out[tp_rank * group_cols:(tp_rank + 1) * group_cols], preferred_element_type=jnp.float32)
        summed = summed + lax.optimization_barrier(head_term.astype(jnp.bfloat16)).astype(jnp.float32)
    return summed.astype(jnp.bfloat16)
```

```python
import functools
import math

import jax
import jax.numpy as jnp
import numpy as np
from jax import lax
from jax.experimental import pallas as pl
from jax.experimental.pallas import tpu as pltpu
from jax.sharding import PartitionSpec as P

H = 32
KVH = 4
HD = 128
EPSILON = 1e-06
ROPE_BASE = 1000000.0
HIDE = 256.0
CHUNKS = 2
MESH = pl.DeviceIdType.MESH
BF16 = jnp.bfloat16
F32 = jnp.float32


def turns_per_token():
    half = HD // 2
    freq = ROPE_BASE ** (-2.0 * np.arange(half) / HD) / (2 * math.pi)
    return np.concatenate([freq, freq])[None, :].astype(np.float32)


def cos_of_turns(turns):
    x = (turns - jnp.round(turns)) * (2 * math.pi)
    x2 = x * x
    out = jnp.full_like(x2, 1.0 / math.factorial(16))
    for n in range(14, -1, -2):
        out = out * x2 + (-1.0) ** (n // 2) / math.factorial(n)
    return out


def mm(a, b):
    return jnp.dot(a, b, preferred_element_type=F32)


def norm_rotate(u, gain, cos2, sin2):
    inv = lax.rsqrt(jnp.mean(u * u, axis=-1, keepdims=True) + EPSILON)
    w = u * inv * gain
    return w * cos2 + pltpu.roll(w, HD // 2, 1) * sin2


def kernel(
    reach, n_ctx, n_tp, docs,
    docs_ref, tok_hbm, wq_hbm, wk_hbm, wv_hbm, wo_hbm, qg_hbm, kg_hbm, fr_hbm,
    out_ref,
    tok, wkv, wq, wo, qg, kg, fr, cos2, sin2, kv, code, q_s, acc, att, s1, r1, s2, r2, own,
    in_sem, wq_sem, z_send, y_send, kv_recv, s1_send, s1_recv, s2_send, s2_recv,
):
    rows = tok.shape[0]
    heads = wq.shape[1] // HD
    wide = code.shape[2]
    chunks, qrows, _ = q_s.shape
    ct = rows // chunks
    nb = n_tp // 2
    cw = out_ref.shape[1]
    i = lax.axis_index("ctx")
    t = lax.axis_index("tp")
    pair = i + 1 - 2 * (i % 2)
    odd = i % 2 == 1
    partner = t + 1 - 2 * (t % 2)
    kv_head = t * heads // (H // KVH)

    def fetch(src, dst, sem):
        copy = pltpu.make_async_copy(src, dst, sem)
        copy.start()
        return copy

    kv_cols = pl.ds(pl.multiple_of(kv_head * HD, HD), HD)
    tok_copy = fetch(tok_hbm, tok, in_sem.at[0])
    wk_copy = fetch(wk_hbm.at[:, kv_cols], wkv.at[:, pl.ds(0, HD)], in_sem.at[1])
    wv_copy = fetch(wv_hbm.at[:, kv_cols], wkv.at[:, pl.ds(HD, HD)], in_sem.at[2])
    small = [
        fetch(fr_hbm, fr, in_sem.at[3]),
        fetch(qg_hbm, qg, in_sem.at[4]),
        fetch(kg_hbm, kg, in_sem.at[5]),
    ]
    q_parts = heads // 2
    wq_copies = [
        fetch(
            wq_hbm.at[:, pl.ds(n * 2 * HD, 2 * HD)],
            wq.at[:, pl.ds(n * 2 * HD, 2 * HD)],
            wq_sem.at[n],
        )
        for n in range(q_parts)
    ]
    wo_copy = fetch(wo_hbm, wo, in_sem.at[6])

    barrier = pltpu.get_barrier_semaphore()

    def greet(where):
        pl.semaphore_signal(barrier, inc=1, device_id=where, device_id_type=MESH)

    greet((pair, t))
    greet((i, partner))
    for step in range(1, nb):
        greet((i, (t + 2 * step) % n_tp))

    @pl.when(i >= 2)
    def _():
        greet((i - 2, t))

    @pl.when(i + 2 < n_ctx)
    def _():
        greet((i + 2, t))

    lane = lax.broadcasted_iota(jnp.int32, (1, wide), 1)

    def add_doc(d, state):
        begin, starts, ends = state
        end = begin + docs_ref[d]
        starts = jnp.where(lane == d, begin, starts)
        ends = jnp.where(lane == d, end, ends)
        return end, starts, ends

    nothing = jnp.full((1, wide), -1, jnp.int32)
    _, starts, ends = lax.fori_loop(0, docs, add_doc, (jnp.int32(0), nothing, nothing))
    local = lax.broadcasted_iota(jnp.int32, (rows, wide), 0)
    lanes = lax.broadcasted_iota(jnp.int32, (rows, wide), 1)

    def members(d):
        pos = local + (i - d) * rows
        return (pos >= starts) & (pos < ends)

    for d in range(reach + 1):
        held = jnp.where(members(d), HIDE, jnp.where(lanes == docs, -HIDE, 0.0))
        code[d] = held.astype(BF16)
    mine = members(0)
    q_code = jnp.where(mine | (lanes == docs), 1.0, 0.0).astype(BF16)
    for c in range(chunks):
        for h in range(heads):
            q_s[c, pl.ds(h * ct, ct), pl.ds(HD, wide)] = q_code[c * ct : (c + 1) * ct]
    start = jnp.sum(jnp.where(mine, starts, 0).astype(F32), axis=1, keepdims=True)
    pos = (lax.broadcasted_iota(jnp.int32, (rows, HD), 0) + i * rows).astype(F32)
    for copy in small:
        copy.wait()
    turns = (pos - start) * fr[...]
    low = lax.broadcasted_iota(jnp.int32, (rows, HD), 1) < HD // 2
    cos2[...] = cos_of_turns(turns)
    sine = cos_of_turns(turns - 0.25)
    sin2[...] = jnp.where(low, -sine, sine)

    for d in range(1, reach + 1):

        @pl.when(i < d)
        def _():
            kv[d] = jnp.zeros(kv.shape[1:], BF16)

    tok_copy.wait()
    wk_copy.wait()
    wv_copy.wait()
    projected = mm(tok[...], wkv[...])
    kv[0, 0] = norm_rotate(projected[:, :HD], kg[...], cos2[...], sin2[...]).astype(BF16)
    kv[0, 1] = projected[:, HD:].astype(BF16)

    greeted = 1 + nb + jnp.where(i >= 2, 1, 0) + jnp.where(i + 2 < n_ctx, 1, 0)
    pl.semaphore_wait(barrier, greeted)

    def hop(src, dst, piece, where, sems):
        return pltpu.make_async_remote_copy(
            src_ref=kv.at[src, piece],
            dst_ref=kv.at[dst, piece],
            send_sem=sems.at[src // 2, piece],
            recv_sem=kv_recv.at[dst, piece],
            device_id=(where, t),
            device_id_type=MESH,
        )

    def hops(d, piece):
        there = i >= d
        moves = []
        if d + 2 <= reach:
            moves.append((there & (i + 2 < n_ctx), hop(d, d + 2, piece, i + 2, z_send)))
        if d + 1 <= reach:
            moves.append((there & jnp.logical_not(odd), hop(d, d + 1, piece, pair, y_send)))
        if d >= 2:
            moves.append((there & odd, hop(d, d - 1, piece, pair, y_send)))
        return moves

    def forward(d):
        for piece in range(2):
            if d:
                arrive(d, piece)
            for cond, copy in hops(d, piece):

                @pl.when(cond)
                def _():
                    copy.start()

    def arrive(d, piece):
        @pl.when(i >= d)
        def _():
            hop(0, d, piece, pair, z_send).wait_recv()

    forward(0)

    scale = HD ** (-0.5) * math.log2(math.e)

    for n in range(q_parts):
        wq_copies[n].wait()

    def project(n, _):
        cols = pl.ds(pl.multiple_of(n * 2 * HD, 2 * HD), 2 * HD)
        both = mm(tok[...], wq[:, cols])
        for k in range(2):
            one = norm_rotate(both[:, k * HD : (k + 1) * HD], qg[...] * scale, cos2[...], sin2[...])
            one = one.astype(BF16)
            at = pl.multiple_of((n * 2 + k) * ct, ct)
            for c in range(chunks):
                q_s[c, pl.ds(at, ct), pl.ds(0, HD)] = one[c * ct : (c + 1) * ct]
        return 0

    lax.fori_loop(0, q_parts, project, 0)
    forward(2)

    group = min(4, heads)
    grows = group * ct
    groups = heads // group
    ones = jnp.ones((rows, HD), BF16)

    def weights_of(c, at, d):
        keys = jnp.concatenate([kv[d, 0], code[d]], axis=1)
        scores = lax.dot_general(
            q_s[c, pl.ds(at, grows), :], keys, (((1,), (1,)), ((), ())), preferred_element_type=F32
        )
        weights = jnp.exp2(scores)
        if d == 0:
            token = lax.broadcasted_iota(jnp.int32, (ct, rows), 0) + c * ct
            seen = lax.broadcasted_iota(jnp.int32, (ct, rows), 1) <= token
            weights = jnp.where(seen[None], weights.reshape(group, ct, rows), 0.0)
            weights = weights.reshape(grows, rows)
        return weights.astype(BF16)

    def weighted(c, at, d):
        return mm(weights_of(c, at, d), jnp.concatenate([kv[d, 1], ones], axis=1))

    def attend(d):
        def step(n, _):
            c = n // groups
            at = pl.multiple_of((n % groups) * grows, grows)
            new = weighted(c, at, d)
            if d == 0:
                acc[c, pl.ds(at, grows), :] = new
            else:
                acc[c, pl.ds(at, grows), :] += new
            return 0

        lax.fori_loop(0, chunks * groups, step, 0)

    attend(0)
    for d in range(2, reach, 2):
        attend(d)
        forward(d + 2)
    for d in range(1, reach - 1, 2):
        for piece in range(2):
            arrive(d, piece)
        attend(d)
    for piece in range(2):
        arrive(reach - 1, piece)

    wo_copy.wait()

    def pair_copy(c, k):
        return pltpu.make_async_remote_copy(
            src_ref=s1.at[c, k],
            dst_ref=r1.at[c, k],
            send_sem=s1_send.at[c, k],
            recv_sem=s1_recv.at[c, k],
            device_id=(i, partner),
            device_id_type=MESH,
        )

    def chip_copy(c, k):
        return pltpu.make_async_remote_copy(
            src_ref=s2.at[c, k - 1],
            dst_ref=r2.at[c, k - 1],
            send_sem=s2_send.at[c, k - 1],
            recv_sem=s2_recv.at[c, k - 1],
            device_id=(i, (t + 2 * k) % n_tp),
            device_id_type=MESH,
        )

    def columns(owner):
        return pl.ds(pl.multiple_of(owner * cw, cw), cw)

    for c in range(chunks):

        def finish(n, _):
            at = pl.multiple_of(n * grows, grows)
            total = acc[c, pl.ds(at, grows), :]
            total = total + weighted(c, at, reach) + weighted(c, at, reach - 1)
            done = (total[:, :HD] / total[:, HD:]).astype(BF16)
            for h in range(group):
                cols = pl.ds(pl.multiple_of(n * group * HD + h * HD, HD), HD)
                att[c, :, cols] = done[h * ct : (h + 1) * ct]
            return 0

        lax.fori_loop(0, groups, finish, 0)
        order = list(range(1, nb)) + [0]
        for k in order:
            s1[c, k] = mm(att[c], wo[:, columns((partner + 2 * k) % n_tp)]).astype(BF16)
            pair_copy(c, k).start()
        for k in order:
            term = mm(att[c], wo[:, columns((t + 2 * k) % n_tp)]).astype(BF16).astype(F32)
            pair_copy(c, k).wait_recv()
            term = term + r1[c, k].astype(F32)
            if k:
                s2[c, k - 1] = term.astype(BF16)
                chip_copy(c, k).start()
            else:
                own[c] = term

    for c in range(chunks):
        total = own[c]
        for k in range(1, nb):
            chip_copy(c, k).wait_recv()
            total = total + r2[c, k - 1].astype(F32)
        out_ref[pl.ds(c * ct, ct), :] = total.astype(out_ref.dtype)

    for c in range(chunks):
        for k in range(nb):
            pair_copy(c, k).wait_send()
            if k:
                chip_copy(c, k).wait_send()
    for d in range(0, reach + 1, 2):
        for piece in range(2):
            for cond, copy in hops(d, piece):

                @pl.when(cond)
                def _():
                    copy.wait_send()


def local(n_ctx, n_tp, tokens, w_query, w_key, w_value, w_out, query_gain, key_gain, doc_lengths):
    rows, width = tokens.shape
    heads = w_query.shape[1] // HD
    out_width = w_out.shape[1]
    reach = min(16, n_ctx // 2)
    docs = doc_lengths.shape[0]
    wide = -(-(docs + 1) // 128) * 128
    chunks = CHUNKS
    ct = rows // chunks
    nb = n_tp // 2
    cw = out_width // n_tp
    dma = pltpu.SemaphoreType.DMA
    anywhere = pl.BlockSpec(memory_space=pl.ANY)
    macs = rows * width * (heads + 2) * HD + rows * heads * HD * out_width
    macs += 2 * rows * heads * rows * (reach + 1) * 2 * HD
    return pl.pallas_call(
        functools.partial(kernel, reach, n_ctx, n_tp, docs),
        out_shape=jax.ShapeDtypeStruct((rows, cw), BF16),
        in_specs=[pl.BlockSpec(memory_space=pltpu.SMEM)] + [anywhere] * 8,
        out_specs=pl.BlockSpec(memory_space=pltpu.VMEM),
        scratch_shapes=[
            pltpu.VMEM((rows, width), BF16),
            pltpu.VMEM((width, 2 * HD), BF16),
            pltpu.VMEM((width, heads * HD), BF16),
            pltpu.VMEM((heads * HD, out_width), BF16),
            pltpu.VMEM((1, HD), F32),
            pltpu.VMEM((1, HD), F32),
            pltpu.VMEM((1, HD), F32),
            pltpu.VMEM((rows, HD), F32),
            pltpu.VMEM((rows, HD), F32),
            pltpu.VMEM((reach + 1, 2, rows, HD), BF16),
            pltpu.VMEM((reach + 1, rows, wide), BF16),
            pltpu.VMEM((chunks, heads * ct, HD + wide), BF16),
            pltpu.VMEM((chunks, heads * ct, 2 * HD), F32),
            pltpu.VMEM((chunks, ct, heads * HD), BF16),
            pltpu.VMEM((chunks, nb, ct, cw), BF16),
            pltpu.VMEM((chunks, nb, ct, cw), BF16),
            pltpu.VMEM((chunks, nb - 1, ct, cw), BF16),
            pltpu.VMEM((chunks, nb - 1, ct, cw), BF16),
            pltpu.VMEM((chunks, ct, cw), F32),
            dma((7,)),
            dma((heads // 2,)),
            dma((reach // 2 + 1, 2)),
            dma((reach // 2 + 1, 2)),
            dma((reach + 1, 2)),
            dma((chunks, nb)),
            dma((chunks, nb)),
            dma((chunks, nb - 1)),
            dma((chunks, nb - 1)),
        ],
        compiler_params=pltpu.CompilerParams(
            collective_id=0, has_side_effects=True, vmem_limit_bytes=48 * 2**20
        ),
        cost_estimate=pl.CostEstimate(
            flops=2 * macs,
            bytes_accessed=2 * (tokens.size + w_query.size + w_out.size + 2 * width * HD),
            transcendentals=rows * heads * rows * (reach + 1),
        ),
        name="attention_layer",
    )(
        doc_lengths, tokens, w_query, w_key, w_value, w_out,
        query_gain.reshape(1, HD), key_gain.reshape(1, HD), jnp.asarray(turns_per_token()),
    )


def solution(mesh):
    return jax.shard_map(
        functools.partial(local, mesh.shape["ctx"], mesh.shape["tp"]),
        mesh=mesh,
        in_specs=(P("ctx", None), P(None, "tp"), P(), P(), P("tp", None), P(), P(), P()),
        out_specs=P("ctx", "tp"),
        check_vma=False,
    )
```

```python
import functools
import math

import jax
import jax.numpy as jnp
import numpy as np
from jax import lax
from jax.experimental import pallas as pl
from jax.experimental.pallas import tpu as pltpu
from jax.sharding import PartitionSpec as P

H = 32
KVH = 4
HD = 128
EPSILON = 1e-06
ROPE_BASE = 1000000.0
HIDE = 256.0
CHUNKS = 2
PIECES = 4
MESH = pl.DeviceIdType.MESH
BF16 = jnp.bfloat16
F32 = jnp.float32


def turns_per_token():
    half = HD // 2
    freq = ROPE_BASE ** (-2.0 * np.arange(half) / HD) / (2 * math.pi)
    return np.concatenate([freq, freq])[None, :].astype(np.float32)


def cos_of_turns(turns):
    x = (turns - jnp.round(turns)) * (2 * math.pi)
    x2 = x * x
    out = jnp.full_like(x2, 1.0 / math.factorial(16))
    for n in range(14, -1, -2):
        out = out * x2 + (-1.0) ** (n // 2) / math.factorial(n)
    return out


def mm(a, b):
    return jnp.dot(a, b, preferred_element_type=F32)


def norm_rotate(u, gain, cos2, sin2):
    inv = lax.rsqrt(jnp.mean(u * u, axis=-1, keepdims=True) + EPSILON)
    w = u * inv * gain
    return w * cos2 + pltpu.roll(w, HD // 2, 1) * sin2


def kernel(
    reach, n_ctx, n_tp, docs,
    docs_ref, tok_hbm, wq_hbm, wk_hbm, wv_hbm, wo_hbm, qg_hbm, kg_hbm, fr_hbm,
    out_ref,
    tok, wkv, wq, wo, qg, kg, fr, cos2, sin2, kv, code, q_s, acc, att, s1, r1, s2, r2, own,
    in_sem, wq_sem, z_send, y_send, kv_recv, s1_send, s1_recv, s2_send, s2_recv,
):
    rows = tok.shape[0]
    heads = wq.shape[1] // HD
    wide = code.shape[2]
    chunks, qrows, _ = q_s.shape
    ct = rows // chunks
    nb = n_tp // 2
    cw = out_ref.shape[1]
    i = lax.axis_index("ctx")
    t = lax.axis_index("tp")
    pair = i + 1 - 2 * (i % 2)
    odd = i % 2 == 1
    partner = t + 1 - 2 * (t % 2)
    kv_head = t * heads // (H // KVH)

    def fetch(src, dst, sem):
        copy = pltpu.make_async_copy(src, dst, sem)
        copy.start()
        return copy

    kv_cols = pl.ds(pl.multiple_of(kv_head * HD, HD), HD)
    tok_copy = fetch(tok_hbm, tok, in_sem.at[0])
    wk_copy = fetch(wk_hbm.at[:, kv_cols], wkv.at[:, pl.ds(0, HD)], in_sem.at[1])
    wv_copy = fetch(wv_hbm.at[:, kv_cols], wkv.at[:, pl.ds(HD, HD)], in_sem.at[2])
    small = [
        fetch(fr_hbm, fr, in_sem.at[3]),
        fetch(qg_hbm, qg, in_sem.at[4]),
        fetch(kg_hbm, kg, in_sem.at[5]),
    ]
    q_parts = heads // 2
    wq_copies = [
        fetch(
            wq_hbm.at[:, pl.ds(n * 2 * HD, 2 * HD)],
            wq.at[:, pl.ds(n * 2 * HD, 2 * HD)],
            wq_sem.at[n],
        )
        for n in range(q_parts)
    ]
    wo_copy = fetch(wo_hbm, wo, in_sem.at[6])

    barrier = pltpu.get_barrier_semaphore()

    def greet(where):
        pl.semaphore_signal(barrier, inc=1, device_id=where, device_id_type=MESH)

    greet((pair, t))
    greet((i, partner))
    for step in range(1, nb):
        greet((i, (t + 2 * step) % n_tp))

    @pl.when(i >= 2)
    def _():
        greet((i - 2, t))

    @pl.when(i + 2 < n_ctx)
    def _():
        greet((i + 2, t))

    lane = lax.broadcasted_iota(jnp.int32, (1, wide), 1)

    def add_doc(d, state):
        begin, starts, ends = state
        end = begin + docs_ref[d]
        starts = jnp.where(lane == d, begin, starts)
        ends = jnp.where(lane == d, end, ends)
        return end, starts, ends

    nothing = jnp.full((1, wide), -1, jnp.int32)
    _, starts, ends = lax.fori_loop(0, docs, add_doc, (jnp.int32(0), nothing, nothing))
    local = lax.broadcasted_iota(jnp.int32, (rows, wide), 0)
    lanes = lax.broadcasted_iota(jnp.int32, (rows, wide), 1)

    def members(d):
        pos = local + (i - d) * rows
        return (pos >= starts) & (pos < ends)

    mine = members(0)
    start = jnp.sum(jnp.where(mine, starts, 0).astype(F32), axis=1, keepdims=True)
    pos = (lax.broadcasted_iota(jnp.int32, (rows, HD), 0) + i * rows).astype(F32)
    for copy in small:
        copy.wait()
    turns = (pos - start) * fr[...]
    low = lax.broadcasted_iota(jnp.int32, (rows, HD), 1) < HD // 2
    cos2[...] = cos_of_turns(turns)
    sine = cos_of_turns(turns - 0.25)
    sin2[...] = jnp.where(low, -sine, sine)

    tok_copy.wait()
    wk_copy.wait()
    wv_copy.wait()
    projected = mm(tok[...], wkv[...])
    kv[0, 0] = norm_rotate(projected[:, :HD], kg[...], cos2[...], sin2[...]).astype(BF16)
    kv[0, 1] = projected[:, HD:].astype(BF16)

    greeted = 1 + nb + jnp.where(i >= 2, 1, 0) + jnp.where(i + 2 < n_ctx, 1, 0)
    pl.semaphore_wait(barrier, greeted)

    part = rows // PIECES

    def hop(src, dst, piece, where, sems):
        here = (slice(None), pl.ds(piece * part, part), slice(None))
        return pltpu.make_async_remote_copy(
            src_ref=kv.at[(src,) + here],
            dst_ref=kv.at[(dst,) + here],
            send_sem=sems.at[src // 2, piece],
            recv_sem=kv_recv.at[dst, piece],
            device_id=(where, t),
            device_id_type=MESH,
        )

    def hops(d, piece):
        there = i >= d
        moves = []
        if d + 2 <= reach:
            moves.append((there & (i + 2 < n_ctx), hop(d, d + 2, piece, i + 2, z_send)))
        if d + 1 <= reach:
            moves.append((there & jnp.logical_not(odd), hop(d, d + 1, piece, pair, y_send)))
        if d >= 2:
            moves.append((there & odd, hop(d, d - 1, piece, pair, y_send)))
        return moves

    def forward(d, pieces):
        for piece in pieces:
            if d:
                arrive(d, piece)
            for cond, copy in hops(d, piece):

                @pl.when(cond)
                def _():
                    copy.start()

    def arrive(d, piece):
        @pl.when(i >= d)
        def _():
            hop(0, d, piece, pair, z_send).wait_recv()

    every = range(PIECES)
    forward(0, every)

    for d in range(reach + 1):
        held = jnp.where(members(d), HIDE, jnp.where(lanes == docs, -HIDE, 0.0))
        code[d] = held.astype(BF16)
    q_code = jnp.where(mine | (lanes == docs), 1.0, 0.0).astype(BF16)
    for c in range(chunks):
        for h in range(heads):
            q_s[c, pl.ds(h * ct, ct), pl.ds(HD, wide)] = q_code[c * ct : (c + 1) * ct]
    for d in range(1, reach + 1):

        @pl.when(i < d)
        def _():
            kv[d] = jnp.zeros(kv.shape[1:], BF16)

    scale = HD ** (-0.5) * math.log2(math.e)

    def project(n, _):
        cols = pl.ds(pl.multiple_of(n * 2 * HD, 2 * HD), 2 * HD)
        both = mm(tok[...], wq[:, cols])
        for k in range(2):
            one = norm_rotate(both[:, k * HD : (k + 1) * HD], qg[...] * scale, cos2[...], sin2[...])
            one = one.astype(BF16)
            at = pl.multiple_of((n * 2 + k) * ct, ct)
            for c in range(chunks):
                q_s[c, pl.ds(at, ct), pl.ds(0, HD)] = one[c * ct : (c + 1) * ct]
        return 0

    early = q_parts - 2
    for n in range(early):
        wq_copies[n].wait()
    lax.fori_loop(0, early, project, 0)
    forward(2, every[:1])
    wq_copies[early].wait()
    project(early, 0)
    forward(2, every[1:2])
    wq_copies[early + 1].wait()
    project(early + 1, 0)
    forward(2, every[2:])

    group = min(4, heads)
    grows = group * ct
    groups = heads // group
    ones = jnp.ones((rows, HD), BF16)

    def weights_of(c, at, d):
        keys = jnp.concatenate([kv[d, 0], code[d]], axis=1)
        scores = lax.dot_general(
            q_s[c, pl.ds(at, grows), :], keys, (((1,), (1,)), ((), ())), preferred_element_type=F32
        )
        weights = jnp.exp2(scores)
        if d == 0:
            token = lax.broadcasted_iota(jnp.int32, (ct, rows), 0) + c * ct
            seen = lax.broadcasted_iota(jnp.int32, (ct, rows), 1) <= token
            weights = jnp.where(seen[None], weights.reshape(group, ct, rows), 0.0)
            weights = weights.reshape(grows, rows)
        return weights.astype(BF16)

    def weighted(c, at, d):
        return mm(weights_of(c, at, d), jnp.concatenate([kv[d, 1], ones], axis=1))

    def attend(d):
        def step(n, _):
            c = n // groups
            at = pl.multiple_of((n % groups) * grows, grows)
            new = weighted(c, at, d)
            if d == 0:
                acc[c, pl.ds(at, grows), :] = new
            else:
                acc[c, pl.ds(at, grows), :] += new
            return 0

        lax.fori_loop(0, chunks * groups, step, 0)

    forward(4, every[:1])
    attend(0)
    forward(4, every[1:])
    attend(2)
    for d in range(6, reach + 1, 2):
        forward(d, every)
        attend(d - 2)
    for d in range(1, reach - 1, 2):
        for piece in every:
            arrive(d, piece)
        attend(d)
    attend(reach)
    for piece in every:
        arrive(reach - 1, piece)

    wo_copy.wait()

    def pair_copy(c, k):
        return pltpu.make_async_remote_copy(
            src_ref=s1.at[c, k],
            dst_ref=r1.at[c, k],
            send_sem=s1_send.at[c, k],
            recv_sem=s1_recv.at[c, k],
            device_id=(i, partner),
            device_id_type=MESH,
        )

    def chip_copy(c, k):
        return pltpu.make_async_remote_copy(
            src_ref=s2.at[c, k - 1],
            dst_ref=r2.at[c, k - 1],
            send_sem=s2_send.at[c, k - 1],
            recv_sem=s2_recv.at[c, k - 1],
            device_id=(i, (t + 2 * k) % n_tp),
            device_id_type=MESH,
        )

    def columns(owner):
        return pl.ds(pl.multiple_of(owner * cw, cw), cw)

    for c in range(chunks):

        def finish(n, _):
            at = pl.multiple_of(n * grows, grows)
            total = acc[c, pl.ds(at, grows), :]
            total = total + weighted(c, at, reach - 1)
            done = (total[:, :HD] / total[:, HD:]).astype(BF16)
            for h in range(group):
                cols = pl.ds(pl.multiple_of(n * group * HD + h * HD, HD), HD)
                att[c, :, cols] = done[h * ct : (h + 1) * ct]
            return 0

        lax.fori_loop(0, groups, finish, 0)
        order = list(range(1, nb)) + [0]
        for k in order:
            s1[c, k] = mm(att[c], wo[:, columns((partner + 2 * k) % n_tp)]).astype(BF16)
            pair_copy(c, k).start()
        for k in order:
            term = mm(att[c], wo[:, columns((t + 2 * k) % n_tp)]).astype(BF16).astype(F32)
            pair_copy(c, k).wait_recv()
            term = term + r1[c, k].astype(F32)
            if k:
                s2[c, k - 1] = term.astype(BF16)
                chip_copy(c, k).start()
            else:
                own[c] = term

    for c in range(chunks):
        total = own[c]
        for k in range(1, nb):
            chip_copy(c, k).wait_recv()
            total = total + r2[c, k - 1].astype(F32)
        out_ref[pl.ds(c * ct, ct), :] = total.astype(out_ref.dtype)

    for c in range(chunks):
        for k in range(nb):
            pair_copy(c, k).wait_send()
            if k:
                chip_copy(c, k).wait_send()
    for d in range(0, reach + 1, 2):
        for piece in every:
            for cond, copy in hops(d, piece):

                @pl.when(cond)
                def _():
                    copy.wait_send()


def local(n_ctx, n_tp, tokens, w_query, w_key, w_value, w_out, query_gain, key_gain, doc_lengths):
    rows, width = tokens.shape
    heads = w_query.shape[1] // HD
    out_width = w_out.shape[1]
    reach = min(16, n_ctx // 2)
    docs = doc_lengths.shape[0]
    wide = -(-(docs + 1) // 128) * 128
    chunks = CHUNKS
    ct = rows // chunks
    nb = n_tp // 2
    cw = out_width // n_tp
    dma = pltpu.SemaphoreType.DMA
    anywhere = pl.BlockSpec(memory_space=pltpu.HBM)
    macs = rows * width * (heads + 2) * HD + rows * heads * HD * out_width
    macs += 2 * rows * heads * rows * (reach + 1) * 2 * HD
    return pl.pallas_call(
        functools.partial(kernel, reach, n_ctx, n_tp, docs),
        out_shape=jax.ShapeDtypeStruct((rows, cw), BF16),
        in_specs=[pl.BlockSpec(memory_space=pltpu.SMEM)] + [anywhere] * 8,
        out_specs=pl.BlockSpec(memory_space=pltpu.VMEM),
        scratch_shapes=[
            pltpu.VMEM((rows, width), BF16),
            pltpu.VMEM((width, 2 * HD), BF16),
            pltpu.VMEM((width, heads * HD), BF16),
            pltpu.VMEM((heads * HD, out_width), BF16),
            pltpu.VMEM((1, HD), F32),
            pltpu.VMEM((1, HD), F32),
            pltpu.VMEM((1, HD), F32),
            pltpu.VMEM((rows, HD), F32),
            pltpu.VMEM((rows, HD), F32),
            pltpu.VMEM((reach + 1, 2, rows, HD), BF16),
            pltpu.VMEM((reach + 1, rows, wide), BF16),
            pltpu.VMEM((chunks, heads * ct, HD + wide), BF16),
            pltpu.VMEM((chunks, heads * ct, 2 * HD), F32),
            pltpu.VMEM((chunks, ct, heads * HD), BF16),
            pltpu.VMEM((chunks, nb, ct, cw), BF16),
            pltpu.VMEM((chunks, nb, ct, cw), BF16),
            pltpu.VMEM((chunks, nb - 1, ct, cw), BF16),
            pltpu.VMEM((chunks, nb - 1, ct, cw), BF16),
            pltpu.VMEM((chunks, ct, cw), F32),
            dma((7,)),
            dma((heads // 2,)),
            dma((reach // 2 + 1, PIECES)),
            dma((reach // 2 + 1, PIECES)),
            dma((reach + 1, PIECES)),
            dma((chunks, nb)),
            dma((chunks, nb)),
            dma((chunks, nb - 1)),
            dma((chunks, nb - 1)),
        ],
        compiler_params=pltpu.CompilerParams(
            collective_id=0, has_side_effects=True, vmem_limit_bytes=64 * 2**20
        ),
        cost_estimate=pl.CostEstimate(
            flops=2 * macs,
            bytes_accessed=2 * (tokens.size + w_query.size + w_out.size + 2 * width * HD),
            transcendentals=rows * heads * rows * (reach + 1),
        ),
        name="attention_layer",
    )(
        doc_lengths, tokens, w_query, w_key, w_value, w_out,
        query_gain.reshape(1, HD), key_gain.reshape(1, HD), jnp.asarray(turns_per_token()),
    )


def solution(mesh):
    return jax.shard_map(
        functools.partial(local, mesh.shape["ctx"], mesh.shape["tp"]),
        mesh=mesh,
        in_specs=(P("ctx", None), P(None, "tp"), P(), P(), P("tp", None), P(), P(), P()),
        out_specs=P("ctx", "tp"),
        check_vma=False,
    )
```

```python
import functools
import math

import jax
import jax.numpy as jnp
import numpy as np
from jax import lax
from jax.experimental import pallas as pl
from jax.experimental.pallas import tpu as pltpu
from jax.sharding import PartitionSpec as P

H = 32
KVH = 4
HD = 128
EPSILON = 1e-06
ROPE_BASE = 1000000.0
HIDE = 256.0
CHUNKS = 4
PIECES = 4
LOADS = 4
MESH = pl.DeviceIdType.MESH
BF16 = jnp.bfloat16
F32 = jnp.float32


def turns_per_token():
    half = HD // 2
    freq = ROPE_BASE ** (-2.0 * np.arange(half) / HD) / (2 * math.pi)
    return np.concatenate([freq, freq])[None, :].astype(np.float32)


def cos_of_turns(turns):
    x = (turns - jnp.round(turns)) * (2 * math.pi)
    x2 = x * x
    out = jnp.full_like(x2, 1.0 / math.factorial(16))
    for n in range(14, -1, -2):
        out = out * x2 + (-1.0) ** (n // 2) / math.factorial(n)
    return out


def mm(a, b):
    return jnp.dot(a, b, preferred_element_type=F32)


def norm_rotate(u, gain, cos2, sin2):
    inv = lax.rsqrt(jnp.mean(u * u, axis=-1, keepdims=True) + EPSILON)
    w = u * inv * gain
    return w * cos2 + pltpu.roll(w, HD // 2, 1) * sin2


def kernel(
    reach, n_ctx, n_tp, docs,
    docs_hbm, tok_hbm, wq_hbm, wk_hbm, wv_hbm, wo_hbm, qg_hbm, kg_hbm, fr_hbm,
    mine_ref, r2,
    docs_ref, tok, wkv, wq, wo, qg, kg, fr, cos2, sin2, kv, kt, q_s, acc, att, s1, r1, s2, own,
    in_sem, tok_sem, wq_sem, own_sem, z_send, y_send, kv_recv, s1_send, s1_recv, s2_send, s2_recv,
):
    rows = tok.shape[0]
    heads = wq.shape[1] // HD
    wide = kt.shape[1] - HD
    chunks, qrows, _ = q_s.shape
    ct = rows // chunks
    nb = n_tp // 2
    cw = mine_ref.shape[1]
    i = lax.axis_index("ctx")
    t = lax.axis_index("tp")
    pair = i + 1 - 2 * (i % 2)
    odd = i % 2 == 1
    partner = t + 1 - 2 * (t % 2)
    kv_head = t * heads // (H // KVH)

    def fetch(src, dst, sem):
        copy = pltpu.make_async_copy(src, dst, sem)
        copy.start()
        return copy

    kv_cols = pl.ds(pl.multiple_of(kv_head * HD, HD), HD)
    small = [
        fetch(docs_hbm, docs_ref, in_sem.at[0]),
        fetch(fr_hbm, fr, in_sem.at[1]),
        fetch(qg_hbm, qg, in_sem.at[2]),
        fetch(kg_hbm, kg, in_sem.at[3]),
    ]
    first = []
    for n in range(LOADS):
        some = pl.ds(n * (rows // LOADS), rows // LOADS)
        first.append(fetch(tok_hbm.at[some], tok.at[some], tok_sem.at[0, n]))
        deep = pl.ds(n * (wkv.shape[0] // LOADS), wkv.shape[0] // LOADS)
        first.append(fetch(wk_hbm.at[deep, kv_cols], wkv.at[deep, pl.ds(0, HD)], tok_sem.at[1, n]))
        first.append(fetch(wv_hbm.at[deep, kv_cols], wkv.at[deep, pl.ds(HD, HD)], tok_sem.at[2, n]))
    q_parts = heads // 2
    wq_copies = [
        fetch(
            wq_hbm.at[:, pl.ds(n * 2 * HD, 2 * HD)],
            wq.at[:, pl.ds(n * 2 * HD, 2 * HD)],
            wq_sem.at[n],
        )
        for n in range(q_parts)
    ]

    barrier = pltpu.get_barrier_semaphore()

    def greet(where):
        pl.semaphore_signal(barrier, inc=1, device_id=where, device_id_type=MESH)

    greet((pair, t))
    greet((i, partner))
    for step in range(1, nb):
        greet((i, (t + 2 * step) % n_tp))

    @pl.when(i >= 2)
    def _():
        greet((i - 2, t))

    @pl.when(i + 2 < n_ctx)
    def _():
        greet((i + 2, t))

    lane = lax.broadcasted_iota(jnp.int32, (1, wide), 1)

    small[0].wait()

    def add_doc(d, state):
        begin, starts, ends = state
        end = begin + docs_ref[d]
        starts = jnp.where(lane == d, begin, starts)
        ends = jnp.where(lane == d, end, ends)
        return end, starts, ends

    nothing = jnp.full((1, wide), -1, jnp.int32)
    _, starts, ends = lax.fori_loop(0, docs, add_doc, (jnp.int32(0), nothing, nothing))
    local = lax.broadcasted_iota(jnp.int32, (rows, wide), 0)
    lanes = lax.broadcasted_iota(jnp.int32, (rows, wide), 1)

    def members(d):
        pos = local + (i - d) * rows
        return (pos >= starts) & (pos < ends)

    mine = members(0)
    start = jnp.sum(jnp.where(mine, starts, 0).astype(F32), axis=1, keepdims=True)
    pos = (lax.broadcasted_iota(jnp.int32, (rows, HD), 0) + i * rows).astype(F32)
    for copy in small[1:]:
        copy.wait()
    turns = (pos - start) * fr[...]
    low = lax.broadcasted_iota(jnp.int32, (rows, HD), 1) < HD // 2
    cos2[...] = cos_of_turns(turns)
    sine = cos_of_turns(turns - 0.25)
    sin2[...] = jnp.where(low, -sine, sine)

    for copy in first:
        copy.wait()
    projected = mm(tok[...], wkv[...])
    kv[0, 0] = norm_rotate(projected[:, :HD], kg[...], cos2[...], sin2[...]).astype(BF16)
    kv[0, 1] = projected[:, HD:].astype(BF16)

    greeted = 1 + nb + jnp.where(i >= 2, 1, 0) + jnp.where(i + 2 < n_ctx, 1, 0)
    pl.semaphore_wait(barrier, greeted)

    part = rows // PIECES

    def hop(src, dst, piece, where, sems):
        here = (slice(None), pl.ds(piece * part, part), slice(None))
        return pltpu.make_async_remote_copy(
            src_ref=kv.at[(src,) + here],
            dst_ref=kv.at[(dst,) + here],
            send_sem=sems.at[src // 2, piece],
            recv_sem=kv_recv.at[dst, piece],
            device_id=(where, t),
            device_id_type=MESH,
        )

    def hops(d, piece):
        there = i >= d
        moves = []
        if d + 2 <= reach:
            moves.append((there & (i + 2 < n_ctx), hop(d, d + 2, piece, i + 2, z_send)))
        if d + 1 <= reach:
            moves.append((there & jnp.logical_not(odd), hop(d, d + 1, piece, pair, y_send)))
        if d >= 2:
            moves.append((there & odd, hop(d, d - 1, piece, pair, y_send)))
        return moves

    def forward(d, pieces):
        for piece in pieces:
            if d:
                arrive(d, piece)
            for cond, copy in hops(d, piece):

                @pl.when(cond)
                def _():
                    copy.start()

    def arrive(d, piece):
        @pl.when(i >= d)
        def _():
            hop(0, d, piece, pair, z_send).wait_recv()

    every = range(PIECES)
    forward(0, every)
    deep = heads * HD // LOADS
    wo_copies = [
        fetch(
            wo_hbm.at[pl.ds(n * deep, deep)], wo.at[pl.ds(n * deep, deep)], in_sem.at[4 + n]
        )
        for n in range(LOADS)
    ]

    for d in range(reach + 1):
        held = jnp.where(members(d), HIDE, jnp.where(lanes == docs, -HIDE, 0.0))
        kt[d, pl.ds(HD, wide), :] = held.T.astype(BF16)
    q_code = jnp.where(mine | (lanes == docs), 1.0, 0.0).astype(BF16)
    for c in range(chunks):
        for h in range(heads):
            q_s[c, pl.ds(h * ct, ct), pl.ds(HD, wide)] = q_code[c * ct : (c + 1) * ct]
    for d in range(1, reach + 1):

        @pl.when(i < d)
        def _():
            kv[d] = jnp.zeros(kv.shape[1:], BF16)

    scale = HD ** (-0.5) * math.log2(math.e)

    def project(n, _):
        cols = pl.ds(pl.multiple_of(n * 2 * HD, 2 * HD), 2 * HD)
        both = mm(tok[...], wq[:, cols])
        for k in range(2):
            one = norm_rotate(both[:, k * HD : (k + 1) * HD], qg[...] * scale, cos2[...], sin2[...])
            one = one.astype(BF16)
            at = pl.multiple_of((n * 2 + k) * ct, ct)
            for c in range(chunks):
                q_s[c, pl.ds(at, ct), pl.ds(0, HD)] = one[c * ct : (c + 1) * ct]
        return 0

    early = q_parts - 2
    for n in range(early):
        wq_copies[n].wait()
    lax.fori_loop(0, early, project, 0)
    forward(2, every[:1])
    wq_copies[early].wait()
    project(early, 0)
    forward(2, every[1:2])
    wq_copies[early + 1].wait()
    project(early + 1, 0)
    forward(2, every[2:])

    group = min(8, heads)
    grows = group * ct
    groups = heads // group
    ones = jnp.ones((rows, HD), BF16)

    def weights_of(c, at, d):
        weights = jnp.exp2(mm(q_s[c, pl.ds(at, grows), :], kt[d]))
        if d == 0:
            token = lax.broadcasted_iota(jnp.int32, (ct, rows), 0) + c * ct
            seen = lax.broadcasted_iota(jnp.int32, (ct, rows), 1) <= token
            weights = jnp.where(seen[None], weights.reshape(group, ct, rows), 0.0)
            weights = weights.reshape(grows, rows)
        return weights.astype(BF16)

    def weighted(c, at, d):
        return mm(weights_of(c, at, d), jnp.concatenate([kv[d, 1], ones], axis=1))

    def turn(d):
        kt[d, pl.ds(0, HD), :] = kv[d, 0].astype(F32).T.astype(BF16)

    def attend(d):
        turn(d)

        def step(n, _):
            c = n // groups
            at = pl.multiple_of((n % groups) * grows, grows)
            new = weighted(c, at, d)
            if d == 0:
                acc[c, pl.ds(at, grows), :] = new
            else:
                acc[c, pl.ds(at, grows), :] += new
            return 0

        lax.fori_loop(0, chunks * groups, step, 0)

    forward(4, every[:1])
    attend(0)
    forward(4, every[1:])
    attend(2)
    for d in range(6, reach + 1, 2):
        forward(d, every)
        attend(d - 2)
    for d in range(1, reach - 1, 2):
        for piece in every:
            arrive(d, piece)
        attend(d)
    turn(reach)
    for piece in every:
        arrive(reach - 1, piece)
    turn(reach - 1)

    for copy in wo_copies:
        copy.wait()

    def pair_copy(c, k):
        return pltpu.make_async_remote_copy(
            src_ref=s1.at[c, k],
            dst_ref=r1.at[c, k],
            send_sem=s1_send.at[c, k],
            recv_sem=s1_recv.at[c, k],
            device_id=(i, partner),
            device_id_type=MESH,
        )

    def chip_copy(c, k):
        return pltpu.make_async_remote_copy(
            src_ref=s2.at[c, k - 1],
            dst_ref=r2.at[k - 1, pl.ds(c * ct, ct)],
            send_sem=s2_send.at[c, k - 1],
            recv_sem=s2_recv.at[c, k - 1],
            device_id=(i, (t + 2 * k) % n_tp),
            device_id_type=MESH,
        )

    def kept(c):
        return pltpu.make_async_copy(own.at[c], mine_ref.at[pl.ds(c * ct, ct)], own_sem.at[c])

    def columns(owner):
        return pl.ds(pl.multiple_of(owner * cw, cw), cw)

    for c in range(chunks):

        def finish(n, _):
            at = pl.multiple_of(n * grows, grows)
            total = acc[c, pl.ds(at, grows), :]
            total = total + weighted(c, at, reach) + weighted(c, at, reach - 1)
            done = (total[:, :HD] / total[:, HD:]).astype(BF16)
            for h in range(group):
                cols = pl.ds(pl.multiple_of(n * group * HD + h * HD, HD), HD)
                att[c, :, cols] = done[h * ct : (h + 1) * ct]
            return 0

        lax.fori_loop(0, groups, finish, 0)
        order = list(range(1, nb)) + [0]
        for k in order:
            s1[c, k] = mm(att[c], wo[:, columns((partner + 2 * k) % n_tp)]).astype(BF16)
            pair_copy(c, k).start()
        for k in order:
            term = mm(att[c], wo[:, columns((t + 2 * k) % n_tp)]).astype(BF16).astype(F32)
            pair_copy(c, k).wait_recv()
            term = term + r1[c, k].astype(F32)
            if k:
                s2[c, k - 1] = term.astype(BF16)
                chip_copy(c, k).start()
            else:
                own[c] = term
                kept(c).start()

    for c in range(chunks):
        kept(c).wait()
        for k in range(1, nb):
            chip_copy(c, k).wait_recv()

    for c in range(chunks):
        for k in range(nb):
            pair_copy(c, k).wait_send()
            if k:
                chip_copy(c, k).wait_send()
    for d in range(0, reach + 1, 2):
        for piece in every:
            for cond, copy in hops(d, piece):

                @pl.when(cond)
                def _():
                    copy.wait_send()


def local(n_ctx, n_tp, tokens, w_query, w_key, w_value, w_out, query_gain, key_gain, doc_lengths):
    rows, width = tokens.shape
    heads = w_query.shape[1] // HD
    out_width = w_out.shape[1]
    reach = min(16, n_ctx // 2)
    docs = doc_lengths.shape[0]
    wide = -(-(docs + 1) // 128) * 128
    chunks = CHUNKS
    ct = rows // chunks
    nb = n_tp // 2
    cw = out_width // n_tp
    dma = pltpu.SemaphoreType.DMA
    anywhere = pl.BlockSpec(memory_space=pltpu.HBM)
    macs = rows * width * (heads + 2) * HD + rows * heads * HD * out_width
    macs += 2 * rows * heads * rows * (reach + 1) * 2 * HD
    mine, others = pl.pallas_call(
        functools.partial(kernel, reach, n_ctx, n_tp, docs),
        out_shape=(
            jax.ShapeDtypeStruct((rows, cw), F32),
            jax.ShapeDtypeStruct((nb - 1, rows, cw), BF16),
        ),
        in_specs=[anywhere] * 9,
        out_specs=(anywhere, anywhere),
        scratch_shapes=[
            pltpu.SMEM((docs,), jnp.int32),
            pltpu.VMEM((rows, width), BF16),
            pltpu.VMEM((width, 2 * HD), BF16),
            pltpu.VMEM((width, heads * HD), BF16),
            pltpu.VMEM((heads * HD, out_width), BF16),
            pltpu.VMEM((1, HD), F32),
            pltpu.VMEM((1, HD), F32),
            pltpu.VMEM((1, HD), F32),
            pltpu.VMEM((rows, HD), F32),
            pltpu.VMEM((rows, HD), F32),
            pltpu.VMEM((reach + 1, 2, rows, HD), BF16),
            pltpu.VMEM((reach + 1, HD + wide, rows), BF16),
            pltpu.VMEM((chunks, heads * ct, HD + wide), BF16),
            pltpu.VMEM((chunks, heads * ct, 2 * HD), F32),
            pltpu.VMEM((chunks, ct, heads * HD), BF16),
            pltpu.VMEM((chunks, nb, ct, cw), BF16),
            pltpu.VMEM((chunks, nb, ct, cw), BF16),
            pltpu.VMEM((chunks, nb - 1, ct, cw), BF16),
            pltpu.VMEM((chunks, ct, cw), F32),
            dma((4 + LOADS,)),
            dma((3, LOADS)),
            dma((heads // 2,)),
            dma((chunks,)),
            dma((reach // 2 + 1, PIECES)),
            dma((reach // 2 + 1, PIECES)),
            dma((reach + 1, PIECES)),
            dma((chunks, nb)),
            dma((chunks, nb)),
            dma((chunks, nb - 1)),
            dma((chunks, nb - 1)),
        ],
        compiler_params=pltpu.CompilerParams(
            collective_id=0, has_side_effects=True, vmem_limit_bytes=64 * 2**20
        ),
        cost_estimate=pl.CostEstimate(
            flops=2 * macs,
            bytes_accessed=2 * (tokens.size + w_query.size + w_out.size + 2 * width * HD),
            transcendentals=rows * heads * rows * (reach + 1),
        ),
        name="attention_layer",
    )(
        doc_lengths, tokens, w_query, w_key, w_value, w_out,
        query_gain.reshape(1, HD), key_gain.reshape(1, HD), jnp.asarray(turns_per_token()),
    )
    return (mine + jnp.sum(others.astype(F32), axis=0)).astype(BF16)


def solution(mesh):
    return jax.shard_map(
        functools.partial(local, mesh.shape["ctx"], mesh.shape["tp"]),
        mesh=mesh,
        in_specs=(P("ctx", None), P(None, "tp"), P(), P(), P("tp", None), P(), P(), P()),
        out_specs=P("ctx", "tp"),
        check_vma=False,
    )
```

```python
import functools
import math

import jax
import jax.numpy as jnp
import numpy as np
from jax import lax
from jax.experimental import pallas as pl
from jax.experimental.pallas import tpu as pltpu
from jax.sharding import PartitionSpec as P

H = 32
KVH = 4
HD = 128
EPSILON = 1e-06
ROPE_BASE = 1000000.0
HIDE = 256.0
CHUNKS = 4
PIECES = 4
LOADS = 4
MESH = pl.DeviceIdType.MESH
BF16 = jnp.bfloat16
F32 = jnp.float32


def turns_per_token():
    half = HD // 2
    freq = ROPE_BASE ** (-2.0 * np.arange(half) / HD) / (2 * math.pi)
    return np.concatenate([freq, freq])[None, :].astype(np.float32)


def cos_of_turns(turns):
    x = (turns - jnp.round(turns)) * (2 * math.pi)
    x2 = x * x
    out = jnp.full_like(x2, 1.0 / math.factorial(16))
    for n in range(14, -1, -2):
        out = out * x2 + (-1.0) ** (n // 2) / math.factorial(n)
    return out


def mm(a, b):
    return jnp.dot(a, b, preferred_element_type=F32)


def norm_rotate(u, gain, cos2, sin2):
    inv = lax.rsqrt(jnp.mean(u * u, axis=-1, keepdims=True) + EPSILON)
    w = u * inv * gain
    return w * cos2 + pltpu.roll(w, HD // 2, 1) * sin2


def kernel(
    reach, n_ctx, n_tp, docs,
    docs_hbm, tok_hbm, wq_hbm, wk_hbm, wv_hbm, wo_hbm, qg_hbm, kg_hbm, fr_hbm,
    mine_ref, r2,
    docs_ref, tok, wkv, wq, wo, qg, kg, fr, cos2, sin2, kv, kt, q_s, acc, att, s1, r1, s2, own,
    in_sem, tok_sem, wq_sem, own_sem, z_send, y_send, kv_recv, s1_send, s1_recv, s2_send, s2_recv,
):
    rows = tok.shape[0]
    heads = wq.shape[1] // HD
    wide = kt.shape[1] - HD
    chunks, qrows, _ = q_s.shape
    ct = rows // chunks
    nb = n_tp // 2
    cw = mine_ref.shape[1]
    i = lax.axis_index("ctx")
    t = lax.axis_index("tp")
    pair = i + 1 - 2 * (i % 2)
    odd = i % 2 == 1
    partner = t + 1 - 2 * (t % 2)
    kv_head = t * heads // (H // KVH)

    def fetch(src, dst, sem):
        copy = pltpu.make_async_copy(src, dst, sem)
        copy.start()
        return copy

    kv_cols = pl.ds(pl.multiple_of(kv_head * HD, HD), HD)
    small = [
        fetch(docs_hbm, docs_ref, in_sem.at[0]),
        fetch(fr_hbm, fr, in_sem.at[1]),
        fetch(qg_hbm, qg, in_sem.at[2]),
        fetch(kg_hbm, kg, in_sem.at[3]),
    ]
    first = []
    for n in range(LOADS):
        some = pl.ds(n * (rows // LOADS), rows // LOADS)
        first.append(fetch(tok_hbm.at[some], tok.at[some], tok_sem.at[0, n]))
        deep = pl.ds(n * (wkv.shape[0] // LOADS), wkv.shape[0] // LOADS)
        first.append(fetch(wk_hbm.at[deep, kv_cols], wkv.at[deep, pl.ds(0, HD)], tok_sem.at[1, n]))
        first.append(fetch(wv_hbm.at[deep, kv_cols], wkv.at[deep, pl.ds(HD, HD)], tok_sem.at[2, n]))
    q_parts = heads // 2

    def wq_copy(n):
        cols = pl.ds(pl.multiple_of(n * 2 * HD, 2 * HD), 2 * HD)
        return pltpu.make_async_copy(wq_hbm.at[:, cols], wq.at[:, cols], wq_sem.at[n])

    for n in range(q_parts):
        wq_copy(n).start()

    barrier = pltpu.get_barrier_semaphore()

    def greet(where):
        pl.semaphore_signal(barrier, inc=1, device_id=where, device_id_type=MESH)

    greet((pair, t))
    greet((i, partner))
    for step in range(1, nb):
        greet((i, (t + 2 * step) % n_tp))

    @pl.when(i >= 2)
    def _():
        greet((i - 2, t))

    @pl.when(i + 2 < n_ctx)
    def _():
        greet((i + 2, t))

    lane = lax.broadcasted_iota(jnp.int32, (1, wide), 1)

    small[0].wait()

    def add_doc(d, state):
        begin, starts, ends = state
        end = begin + docs_ref[d]
        starts = jnp.where(lane == d, begin, starts)
        ends = jnp.where(lane == d, end, ends)
        return end, starts, ends

    nothing = jnp.full((1, wide), -1, jnp.int32)
    _, starts, ends = lax.fori_loop(0, docs, add_doc, (jnp.int32(0), nothing, nothing))
    local = lax.broadcasted_iota(jnp.int32, (rows, wide), 0)
    lanes = lax.broadcasted_iota(jnp.int32, (rows, wide), 1)

    def members(d):
        pos = local + (i - d) * rows
        return (pos >= starts) & (pos < ends)

    mine = members(0)
    start = jnp.sum(jnp.where(mine, starts, 0).astype(F32), axis=1, keepdims=True)
    pos = (lax.broadcasted_iota(jnp.int32, (rows, HD), 0) + i * rows).astype(F32)
    for copy in small[1:]:
        copy.wait()
    turns = (pos - start) * fr[...]
    low = lax.broadcasted_iota(jnp.int32, (rows, HD), 1) < HD // 2
    cos2[...] = cos_of_turns(turns)
    sine = cos_of_turns(turns - 0.25)
    sin2[...] = jnp.where(low, -sine, sine)

    for copy in first:
        copy.wait()
    projected = mm(tok[...], wkv[...])
    kv[0, 0] = norm_rotate(projected[:, :HD], kg[...], cos2[...], sin2[...]).astype(BF16)
    kv[0, 1] = projected[:, HD:].astype(BF16)

    greeted = 1 + nb + jnp.where(i >= 2, 1, 0) + jnp.where(i + 2 < n_ctx, 1, 0)
    pl.semaphore_wait(barrier, greeted)

    part = rows // PIECES

    def hop(src, dst, piece, where, sems):
        here = (slice(None), pl.ds(pl.multiple_of(piece * part, part), part), slice(None))
        return pltpu.make_async_remote_copy(
            src_ref=kv.at[(src,) + here],
            dst_ref=kv.at[(dst,) + here],
            send_sem=sems.at[src // 2, piece],
            recv_sem=kv_recv.at[dst, piece],
            device_id=(where, t),
            device_id_type=MESH,
        )

    def hops(d, piece):
        there = i >= d
        moves = []
        if d + 2 <= reach:
            moves.append((there & (i + 2 < n_ctx), hop(d, d + 2, piece, i + 2, z_send)))
        if d + 1 <= reach:
            moves.append((there & jnp.logical_not(odd), hop(d, d + 1, piece, pair, y_send)))
        if d >= 2:
            moves.append((there & odd, hop(d, d - 1, piece, pair, y_send)))
        return moves

    def forward(d, pieces):
        for piece in pieces:
            if d:
                arrive(d, piece)
            for cond, copy in hops(d, piece):

                @pl.when(cond)
                def _():
                    copy.start()

    def arrive(d, piece):
        @pl.when(i >= d)
        def _():
            hop(0, d, piece, pair, z_send).wait_recv()

    every = range(PIECES)
    forward(0, every)
    deep = heads * HD // LOADS
    wo_copies = [
        fetch(
            wo_hbm.at[pl.ds(n * deep, deep)], wo.at[pl.ds(n * deep, deep)], in_sem.at[4 + n]
        )
        for n in range(LOADS)
    ]

    for d in range(reach + 1):
        held = jnp.where(members(d), HIDE, jnp.where(lanes == docs, -HIDE, 0.0))
        kt[d, pl.ds(HD, wide), :] = held.T.astype(BF16)
    q_code = jnp.where(mine | (lanes == docs), 1.0, 0.0).astype(BF16)
    for c in range(chunks):
        for h in range(heads):
            q_s[c, pl.ds(h * ct, ct), pl.ds(HD, wide)] = q_code[c * ct : (c + 1) * ct]
    for d in range(1, reach + 1):

        @pl.when(i < d)
        def _():
            kv[d] = jnp.zeros(kv.shape[1:], BF16)

    scale = HD ** (-0.5) * math.log2(math.e)

    def project(n, _):
        cols = pl.ds(pl.multiple_of(n * 2 * HD, 2 * HD), 2 * HD)
        both = mm(tok[...], wq[:, cols])
        for k in range(2):
            one = norm_rotate(both[:, k * HD : (k + 1) * HD], qg[...] * scale, cos2[...], sin2[...])
            one = one.astype(BF16)
            at = pl.multiple_of((n * 2 + k) * ct, ct)
            for c in range(chunks):
                q_s[c, pl.ds(at, ct), pl.ds(0, HD)] = one[c * ct : (c + 1) * ct]
        return 0

    def query_part(n, _):
        wq_copy(n).wait()
        project(n, 0)

        @pl.when(n >= 1)
        def _():
            forward(2, [n - 1])

        return 0

    lax.fori_loop(0, q_parts, query_part, 0)
    forward(2, every[q_parts - 1 :])

    group = min(8, heads)
    grows = group * ct
    groups = heads // group
    ones = jnp.ones((rows, HD), BF16)

    def weights_of(c, at, d):
        weights = jnp.exp2(mm(q_s[c, pl.ds(at, grows), :], kt[d]))
        if d == 0:
            token = lax.broadcasted_iota(jnp.int32, (ct, rows), 0) + c * ct
            seen = lax.broadcasted_iota(jnp.int32, (ct, rows), 1) <= token
            weights = jnp.where(seen[None], weights.reshape(group, ct, rows), 0.0)
            weights = weights.reshape(grows, rows)
        return weights.astype(BF16)

    def weighted(c, at, d):
        return mm(weights_of(c, at, d), jnp.concatenate([kv[d, 1], ones], axis=1))

    def turn(d):
        kt[d, pl.ds(0, HD), :] = kv[d, 0].astype(F32).T.astype(BF16)

    def attend(d):
        turn(d)

        def step(n, _):
            c = n // groups
            at = pl.multiple_of((n % groups) * grows, grows)
            new = weighted(c, at, d)
            if d == 0:
                acc[c, pl.ds(at, grows), :] = new
            else:
                acc[c, pl.ds(at, grows), :] += new
            return 0

        lax.fori_loop(0, chunks * groups, step, 0)

    forward(4, every[:1])
    attend(0)
    forward(4, every[1:])
    attend(2)
    for d in range(6, reach + 1, 2):
        forward(d, every)
        attend(d - 2)
    for d in range(1, reach - 1, 2):
        for piece in every:
            arrive(d, piece)
        attend(d)
    turn(reach)
    for piece in every:
        arrive(reach - 1, piece)
    turn(reach - 1)

    for copy in wo_copies:
        copy.wait()

    def pair_copy(c, k):
        return pltpu.make_async_remote_copy(
            src_ref=s1.at[c, k],
            dst_ref=r1.at[c, k],
            send_sem=s1_send.at[c, k],
            recv_sem=s1_recv.at[c, k],
            device_id=(i, partner),
            device_id_type=MESH,
        )

    def chip_copy(c, k):
        return pltpu.make_async_remote_copy(
            src_ref=s2.at[c, k - 1],
            dst_ref=r2.at[k - 1, pl.ds(pl.multiple_of(c * ct, ct), ct)],
            send_sem=s2_send.at[c, k - 1],
            recv_sem=s2_recv.at[c, k - 1],
            device_id=(i, (t + 2 * k) % n_tp),
            device_id_type=MESH,
        )

    def kept(c):
        return pltpu.make_async_copy(
            own.at[c, 0], mine_ref.at[pl.ds(pl.multiple_of(c * ct, ct), ct)], own_sem.at[c]
        )

    def columns(owner):
        return pl.ds(pl.multiple_of(owner * cw, cw), cw)

    def finish(c):
        def step(n, _):
            at = pl.multiple_of(n * grows, grows)
            total = acc[c, pl.ds(at, grows), :]
            total = total + weighted(c, at, reach) + weighted(c, at, reach - 1)
            done = (total[:, :HD] / total[:, HD:]).astype(BF16)
            for h in range(group):
                cols = pl.ds(pl.multiple_of(n * group * HD + h * HD, HD), HD)
                att[:, cols] = done[h * ct : (h + 1) * ct]
            return 0

        if groups == 1:
            step(0, 0)
        else:
            lax.fori_loop(0, groups, step, 0)

    order = list(range(1, nb)) + [0]

    def pair_sum(c):
        for k in order:
            pair_copy(c, k).wait_recv()
            term = own[c, k] + r1[c, k].astype(F32)
            if k:
                s2[c, k - 1] = term.astype(BF16)
                chip_copy(c, k).start()
            else:
                own[c, 0] = term
                kept(c).start()

    def chunk(c, _):
        finish(c)

        @pl.when(c >= 1)
        def _():
            pair_sum(c - 1)

        for k in order:
            s1[c, k] = mm(att[...], wo[:, columns((partner + 2 * k) % n_tp)]).astype(BF16)
            pair_copy(c, k).start()
        for k in order:
            term = mm(att[...], wo[:, columns((t + 2 * k) % n_tp)])
            own[c, k] = term.astype(BF16).astype(F32)
        return 0

    lax.fori_loop(0, chunks, chunk, 0)
    pair_sum(chunks - 1)

    for c in range(chunks):
        kept(c).wait()
        for k in range(1, nb):
            chip_copy(c, k).wait_recv()

    for c in range(chunks):
        for k in range(nb):
            pair_copy(c, k).wait_send()
            if k:
                chip_copy(c, k).wait_send()
    for d in range(0, reach + 1, 2):
        for piece in every:
            for cond, copy in hops(d, piece):

                @pl.when(cond)
                def _():
                    copy.wait_send()


def local(n_ctx, n_tp, tokens, w_query, w_key, w_value, w_out, query_gain, key_gain, doc_lengths):
    rows, width = tokens.shape
    heads = w_query.shape[1] // HD
    out_width = w_out.shape[1]
    reach = min(16, n_ctx // 2)
    docs = doc_lengths.shape[0]
    wide = -(-(docs + 1) // 128) * 128
    chunks = CHUNKS
    ct = rows // chunks
    nb = n_tp // 2
    cw = out_width // n_tp
    dma = pltpu.SemaphoreType.DMA
    anywhere = pl.BlockSpec(memory_space=pltpu.HBM)
    macs = rows * width * (heads + 2) * HD + rows * heads * HD * out_width
    macs += 2 * rows * heads * rows * (reach + 1) * 2 * HD
    mine, others = pl.pallas_call(
        functools.partial(kernel, reach, n_ctx, n_tp, docs),
        out_shape=(
            jax.ShapeDtypeStruct((rows, cw), F32),
            jax.ShapeDtypeStruct((nb - 1, rows, cw), BF16),
        ),
        in_specs=[anywhere] * 9,
        out_specs=(anywhere, anywhere),
        scratch_shapes=[
            pltpu.SMEM((docs,), jnp.int32),
            pltpu.VMEM((rows, width), BF16),
            pltpu.VMEM((width, 2 * HD), BF16),
            pltpu.VMEM((width, heads * HD), BF16),
            pltpu.VMEM((heads * HD, out_width), BF16),
            pltpu.VMEM((1, HD), F32),
            pltpu.VMEM((1, HD), F32),
            pltpu.VMEM((1, HD), F32),
            pltpu.VMEM((rows, HD), F32),
            pltpu.VMEM((rows, HD), F32),
            pltpu.VMEM((reach + 1, 2, rows, HD), BF16),
            pltpu.VMEM((reach + 1, HD + wide, rows), BF16),
            pltpu.VMEM((chunks, heads * ct, HD + wide), BF16),
            pltpu.VMEM((chunks, heads * ct, 2 * HD), F32),
            pltpu.VMEM((ct, heads * HD), BF16),
            pltpu.VMEM((chunks, nb, ct, cw), BF16),
            pltpu.VMEM((chunks, nb, ct, cw), BF16),
            pltpu.VMEM((chunks, nb - 1, ct, cw), BF16),
            pltpu.VMEM((chunks, nb, ct, cw), F32),
            dma((4 + LOADS,)),
            dma((3, LOADS)),
            dma((heads // 2,)),
            dma((chunks,)),
            dma((reach // 2 + 1, PIECES)),
            dma((reach // 2 + 1, PIECES)),
            dma((reach + 1, PIECES)),
            dma((chunks, nb)),
            dma((chunks, nb)),
            dma((chunks, nb - 1)),
            dma((chunks, nb - 1)),
        ],
        compiler_params=pltpu.CompilerParams(
            collective_id=0, has_side_effects=True, vmem_limit_bytes=64 * 2**20
        ),
        cost_estimate=pl.CostEstimate(
            flops=2 * macs,
            bytes_accessed=2 * (tokens.size + w_query.size + w_out.size + 2 * width * HD),
            transcendentals=rows * heads * rows * (reach + 1),
        ),
        name="attention_layer",
    )(
        doc_lengths, tokens, w_query, w_key, w_value, w_out,
        query_gain.reshape(1, HD), key_gain.reshape(1, HD), jnp.asarray(turns_per_token()),
    )
    return (mine + jnp.sum(others.astype(F32), axis=0)).astype(BF16)


def solution(mesh):
    return jax.shard_map(
        functools.partial(local, mesh.shape["ctx"], mesh.shape["tp"]),
        mesh=mesh,
        in_specs=(P("ctx", None), P(None, "tp"), P(), P(), P("tp", None), P(), P(), P()),
        out_specs=P("ctx", "tp"),
        check_vma=False,
    )
```

```python
import functools
import math

import jax
import jax.numpy as jnp
import numpy as np
from jax import lax
from jax.experimental import pallas as pl
from jax.experimental.pallas import tpu as pltpu
from jax.sharding import PartitionSpec as P

H = 32
KVH = 4
HD = 128
EPSILON = 1e-06
ROPE_BASE = 1000000.0
HIDE = 256.0
CHUNKS = 4
PIECES = 4
LOADS = 4
MESH = pl.DeviceIdType.MESH
BF16 = jnp.bfloat16
F32 = jnp.float32


def turns_per_token():
    half = HD // 2
    freq = ROPE_BASE ** (-2.0 * np.arange(half) / HD) / (2 * math.pi)
    return np.concatenate([freq, freq])[None, :].astype(np.float32)


def cos_of_turns(turns):
    x = (turns - jnp.round(turns)) * (2 * math.pi)
    x2 = x * x
    out = jnp.full_like(x2, 1.0 / math.factorial(16))
    for n in range(14, -1, -2):
        out = out * x2 + (-1.0) ** (n // 2) / math.factorial(n)
    return out


def mm(a, b):
    return jnp.dot(a, b, preferred_element_type=F32)


def norm_rotate(u, gain, cos2, sin2):
    inv = lax.rsqrt(jnp.mean(u * u, axis=-1, keepdims=True) + EPSILON)
    w = u * inv * gain
    return w * cos2 + pltpu.roll(w, HD // 2, 1) * sin2


def kernel(
    reach, n_ctx, n_tp, docs,
    docs_hbm, tok_hbm, wq_hbm, wk_hbm, wv_hbm, wo_hbm, qg_hbm, kg_hbm, fr_hbm,
    mine_ref, r2,
    docs_ref, tok, wkv, wq, wo, qg, kg, fr, cos2, sin2, kv, kt, vt, q_s, acc, att, s1, r1, s2, s1_own, r1_own, own,
    in_sem, tok_sem, wq_sem, own_sem, z_send, y_send, kv_recv, s1_send, s1_recv, s2_send, s2_recv,
):
    rows = tok.shape[0]
    heads = wq.shape[1] // HD
    wide = kt.shape[1] - HD
    chunks, qrows, _ = q_s.shape
    ct = rows // chunks
    nb = n_tp // 2
    cw = mine_ref.shape[1]
    i = lax.axis_index("ctx")
    t = lax.axis_index("tp")
    pair = i + 1 - 2 * (i % 2)
    odd = i % 2 == 1
    partner = t + 1 - 2 * (t % 2)
    kv_head = t * heads // (H // KVH)

    def fetch(src, dst, sem):
        copy = pltpu.make_async_copy(src, dst, sem)
        copy.start()
        return copy

    kv_cols = pl.ds(pl.multiple_of(kv_head * HD, HD), HD)
    small = [
        fetch(docs_hbm, docs_ref, in_sem.at[0]),
        fetch(fr_hbm, fr, in_sem.at[1]),
        fetch(qg_hbm, qg, in_sem.at[2]),
        fetch(kg_hbm, kg, in_sem.at[3]),
    ]
    first = []
    for n in range(LOADS):
        some = pl.ds(n * (rows // LOADS), rows // LOADS)
        first.append(fetch(tok_hbm.at[some], tok.at[some], tok_sem.at[0, n]))
        deep = pl.ds(n * (wkv.shape[0] // LOADS), wkv.shape[0] // LOADS)
        first.append(fetch(wk_hbm.at[deep, kv_cols], wkv.at[deep, pl.ds(0, HD)], tok_sem.at[1, n]))
        first.append(fetch(wv_hbm.at[deep, kv_cols], wkv.at[deep, pl.ds(HD, HD)], tok_sem.at[2, n]))
    q_parts = heads // 2

    def wq_copy(n):
        cols = pl.ds(pl.multiple_of(n * 2 * HD, 2 * HD), 2 * HD)
        return pltpu.make_async_copy(wq_hbm.at[:, cols], wq.at[:, cols], wq_sem.at[n])

    for n in range(q_parts):
        wq_copy(n).start()

    barrier = pltpu.get_barrier_semaphore()

    def greet(where):
        pl.semaphore_signal(barrier, inc=1, device_id=where, device_id_type=MESH)

    greet((pair, t))
    greet((i, partner))
    for step in range(1, nb):
        greet((i, (t + 2 * step) % n_tp))

    @pl.when(i >= 2)
    def _():
        greet((i - 2, t))

    @pl.when(i + 2 < n_ctx)
    def _():
        greet((i + 2, t))

    lane = lax.broadcasted_iota(jnp.int32, (1, wide), 1)

    small[0].wait()

    def add_doc(d, state):
        begin, starts, ends = state
        end = begin + docs_ref[d]
        starts = jnp.where(lane == d, begin, starts)
        ends = jnp.where(lane == d, end, ends)
        return end, starts, ends

    nothing = jnp.full((1, wide), -1, jnp.int32)
    _, starts, ends = lax.fori_loop(0, docs, add_doc, (jnp.int32(0), nothing, nothing))
    local = lax.broadcasted_iota(jnp.int32, (rows, wide), 0)
    lanes = lax.broadcasted_iota(jnp.int32, (rows, wide), 1)

    def nth(j):
        if j == 0:
            return 0
        return j + (1 - i % 2) * (1 if j % 2 else -1)

    def members(d):
        pos = local + (i - d) * rows
        return (pos >= starts) & (pos < ends)

    mine = members(0)
    start = jnp.sum(jnp.where(mine, starts, 0).astype(F32), axis=1, keepdims=True)
    pos = (lax.broadcasted_iota(jnp.int32, (rows, HD), 0) + i * rows).astype(F32)
    for copy in small[1:]:
        copy.wait()
    turns = (pos - start) * fr[...]
    low = lax.broadcasted_iota(jnp.int32, (rows, HD), 1) < HD // 2
    cos2[...] = cos_of_turns(turns)
    sine = cos_of_turns(turns - 0.25)
    sin2[...] = jnp.where(low, -sine, sine)

    for copy in first:
        copy.wait()
    projected = mm(tok[...], wkv[...])
    kv[0, 0] = norm_rotate(projected[:, :HD], kg[...], cos2[...], sin2[...]).astype(BF16)
    kv[0, 1] = projected[:, HD:].astype(BF16)

    greeted = 1 + nb + jnp.where(i >= 2, 1, 0) + jnp.where(i + 2 < n_ctx, 1, 0)
    pl.semaphore_wait(barrier, greeted)

    part = rows // PIECES

    def hop(src, dst, piece, where, sems):
        here = (slice(None), pl.ds(pl.multiple_of(piece * part, part), part), slice(None))
        return pltpu.make_async_remote_copy(
            src_ref=kv.at[(src,) + here],
            dst_ref=kv.at[(dst,) + here],
            send_sem=sems.at[src // 2, piece],
            recv_sem=kv_recv.at[dst, piece],
            device_id=(where, t),
            device_id_type=MESH,
        )

    def hops(d, piece):
        there = i >= d
        moves = []
        if d + 2 <= reach:
            moves.append((there & (i + 2 < n_ctx), hop(d, d + 2, piece, i + 2, z_send)))
        if d + 1 <= reach:
            moves.append((there & jnp.logical_not(odd), hop(d, d + 1, piece, pair, y_send)))
        if d >= 2:
            moves.append((there & odd, hop(d, d - 1, piece, pair, y_send)))
        return moves

    def forward(d, pieces):
        for piece in pieces:
            if d:
                arrive(d, piece)
            for cond, copy in hops(d, piece):

                @pl.when(cond)
                def _():
                    copy.start()

    def arrive(d, piece):
        @pl.when(i >= d)
        def _():
            hop(0, d, piece, pair, z_send).wait_recv()

    every = range(PIECES)
    forward(0, every)
    deep = heads * HD // LOADS
    wo_copies = [
        fetch(
            wo_hbm.at[pl.ds(n * deep, deep)], wo.at[pl.ds(n * deep, deep)], in_sem.at[4 + n]
        )
        for n in range(LOADS)
    ]

    for d in range(reach + 1):
        vt[d, :, pl.ds(HD, HD)] = jnp.ones((rows, HD), BF16)
        held = jnp.where(members(nth(d)), HIDE, jnp.where(lanes == docs, -HIDE, 0.0))
        kt[d, pl.ds(HD, wide), :] = held.T.astype(BF16)
    q_code = jnp.where(mine | (lanes == docs), 1.0, 0.0).astype(BF16)
    for c in range(chunks):
        for h in range(heads):
            q_s[c, pl.ds(h * ct, ct), pl.ds(HD, wide)] = q_code[c * ct : (c + 1) * ct]
    for d in range(1, reach + 1):

        @pl.when(i < d)
        def _():
            kv[d] = jnp.zeros(kv.shape[1:], BF16)

    scale = HD ** (-0.5) * math.log2(math.e)

    def project(n, _):
        cols = pl.ds(pl.multiple_of(n * 2 * HD, 2 * HD), 2 * HD)
        both = mm(tok[...], wq[:, cols])
        for k in range(2):
            one = norm_rotate(both[:, k * HD : (k + 1) * HD], qg[...] * scale, cos2[...], sin2[...])
            one = one.astype(BF16)
            at = pl.multiple_of((n * 2 + k) * ct, ct)
            for c in range(chunks):
                q_s[c, pl.ds(at, ct), pl.ds(0, HD)] = one[c * ct : (c + 1) * ct]
        return 0

    def query_part(n, _):
        wq_copy(n).wait()
        project(n, 0)

        @pl.when(n >= 1)
        def _():
            forward(2, [n - 1])

        return 0

    lax.fori_loop(0, q_parts, query_part, 0)
    forward(2, every[q_parts - 1 :])

    group = min(8, heads)
    grows = group * ct
    groups = heads // group

    def weights_of(c, at, d, first):
        weights = jnp.exp2(mm(q_s[c, pl.ds(at, grows), :], kt[d]))
        if first:
            token = lax.broadcasted_iota(jnp.int32, (ct, rows), 0) + c * ct
            seen = lax.broadcasted_iota(jnp.int32, (ct, rows), 1) <= token
            weights = jnp.where(seen[None], weights.reshape(group, ct, rows), 0.0)
            weights = weights.reshape(grows, rows)
        return weights.astype(BF16)

    def weighted(c, at, d, first=False):
        return mm(weights_of(c, at, d, first), vt[d])

    def place(j, d):
        if d % 2:

            @pl.when(i >= d)
            def _():
                for piece in every:
                    hop(0, d, piece, pair, z_send).wait_recv()

        kt[j, pl.ds(0, HD), :] = kv[d, 0].astype(F32).T.astype(BF16)
        vt[j, :, pl.ds(0, HD)] = kv[d, 1]

    def turn(j):
        if j == 0:
            place(0, 0)
            return

        @pl.when(odd)
        def _():
            place(j, j)

        @pl.when(jnp.logical_not(odd))
        def _():
            place(j, j + 1 if j % 2 else j - 1)

    def attend(d, first=False):
        turn(d)

        def step(n, _):
            c = n // groups
            at = pl.multiple_of((n % groups) * grows, grows)
            new = weighted(c, at, d, first)
            if first:
                acc[c, pl.ds(at, grows), :] = new
            else:
                acc[c, pl.ds(at, grows), :] += new
            return 0

        lax.fori_loop(0, chunks * groups, step, 0)

    forward(4, every[:1])
    attend(0, True)
    forward(4, every[1:])
    for j in range(1, reach):
        if j > 2 and j % 2 and j + 3 <= reach:
            forward(j + 3, every)
        attend(j)
    turn(reach)

    for copy in wo_copies:
        copy.wait()

    def some_rows(c):
        return pl.ds(pl.multiple_of(c * ct, ct), ct)

    def pair_copy(c, k):
        return pltpu.make_async_remote_copy(
            src_ref=s1.at[c, k - 1],
            dst_ref=r1.at[c, k - 1],
            send_sem=s1_send.at[c, k],
            recv_sem=s1_recv.at[c, k],
            device_id=(i, partner),
            device_id_type=MESH,
        )

    def chip_copy(c, k):
        return pltpu.make_async_remote_copy(
            src_ref=s2.at[c, k - 1],
            dst_ref=r2.at[k - 1, some_rows(c)],
            send_sem=s2_send.at[c, k - 1],
            recv_sem=s2_recv.at[c, k - 1],
            device_id=(i, (t + 2 * k) % n_tp),
            device_id_type=MESH,
        )

    own_copy = pltpu.make_async_remote_copy(
        src_ref=s1_own,
        dst_ref=r1_own,
        send_sem=s1_send.at[0, 0],
        recv_sem=s1_recv.at[0, 0],
        device_id=(i, partner),
        device_id_type=MESH,
    )
    kept = pltpu.make_async_copy(own.at[0], mine_ref, own_sem.at[0])

    def columns(owner):
        return pl.ds(pl.multiple_of(owner * cw, cw), cw)

    def finish(c):
        def step(n, _):
            at = pl.multiple_of(n * grows, grows)
            total = acc[c, pl.ds(at, grows), :] + weighted(c, at, reach)
            done = (total[:, :HD] / total[:, HD:]).astype(BF16)
            for h in range(group):
                cols = pl.ds(pl.multiple_of(n * group * HD + h * HD, HD), HD)
                att[some_rows(c), cols] = done[h * ct : (h + 1) * ct]
            return 0

        if groups == 1:
            step(0, 0)
        else:
            lax.fori_loop(0, groups, step, 0)

    def pair_sum(c):
        for k in range(1, nb):
            pair_copy(c, k).wait_recv()
            term = own[k, some_rows(c)] + r1[c, k - 1].astype(F32)
            s2[c, k - 1] = term.astype(BF16)
            chip_copy(c, k).start()

    def chunk(c, _):
        finish(c)

        @pl.when(c >= 1)
        def _():
            pair_sum(c - 1)

        for k in range(1, nb):
            term = mm(att[some_rows(c)], wo[:, columns((partner + 2 * k) % n_tp)])
            s1[c, k - 1] = term.astype(BF16)
            pair_copy(c, k).start()
        for k in range(1, nb):
            term = mm(att[some_rows(c)], wo[:, columns((t + 2 * k) % n_tp)])
            own[k, some_rows(c)] = term.astype(BF16).astype(F32)
        return 0

    lax.fori_loop(0, chunks, chunk, 0)
    pair_sum(chunks - 1)
    s1_own[...] = mm(att[...], wo[:, columns(partner)]).astype(BF16)
    own_copy.start()
    own[0] = mm(att[...], wo[:, columns(t)]).astype(BF16).astype(F32)
    own_copy.wait_recv()
    own[0] += r1_own[...].astype(F32)
    kept.start()
    kept.wait()
    for c in range(chunks):
        for k in range(1, nb):
            chip_copy(c, k).wait_recv()

    own_copy.wait_send()
    for c in range(chunks):
        for k in range(1, nb):
            pair_copy(c, k).wait_send()
            chip_copy(c, k).wait_send()
    for d in range(0, reach + 1, 2):
        for piece in every:
            for cond, copy in hops(d, piece):

                @pl.when(cond)
                def _():
                    copy.wait_send()


def local(n_ctx, n_tp, tokens, w_query, w_key, w_value, w_out, query_gain, key_gain, doc_lengths):
    rows, width = tokens.shape
    heads = w_query.shape[1] // HD
    out_width = w_out.shape[1]
    reach = min(16, n_ctx // 2)
    docs = doc_lengths.shape[0]
    wide = -(-(docs + 1) // 128) * 128
    chunks = CHUNKS
    ct = rows // chunks
    nb = n_tp // 2
    cw = out_width // n_tp
    dma = pltpu.SemaphoreType.DMA
    anywhere = pl.BlockSpec(memory_space=pltpu.HBM)
    macs = rows * width * (heads + 2) * HD + rows * heads * HD * out_width
    macs += 2 * rows * heads * rows * (reach + 1) * 2 * HD
    mine, others = pl.pallas_call(
        functools.partial(kernel, reach, n_ctx, n_tp, docs),
        out_shape=(
            jax.ShapeDtypeStruct((rows, cw), F32),
            jax.ShapeDtypeStruct((nb - 1, rows, cw), BF16),
        ),
        in_specs=[anywhere] * 9,
        out_specs=(anywhere, anywhere),
        scratch_shapes=[
            pltpu.SMEM((docs,), jnp.int32),
            pltpu.VMEM((rows, width), BF16),
            pltpu.VMEM((width, 2 * HD), BF16),
            pltpu.VMEM((width, heads * HD), BF16),
            pltpu.VMEM((heads * HD, out_width), BF16),
            pltpu.VMEM((1, HD), F32),
            pltpu.VMEM((1, HD), F32),
            pltpu.VMEM((1, HD), F32),
            pltpu.VMEM((rows, HD), F32),
            pltpu.VMEM((rows, HD), F32),
            pltpu.VMEM((reach + 1, 2, rows, HD), BF16),
            pltpu.VMEM((reach + 1, HD + wide, rows), BF16),
            pltpu.VMEM((reach + 1, rows, 2 * HD), BF16),
            pltpu.VMEM((chunks, heads * ct, HD + wide), BF16),
            pltpu.VMEM((chunks, heads * ct, 2 * HD), F32),
            pltpu.VMEM((rows, heads * HD), BF16),
            pltpu.VMEM((chunks, nb - 1, ct, cw), BF16),
            pltpu.VMEM((chunks, nb - 1, ct, cw), BF16),
            pltpu.VMEM((chunks, nb - 1, ct, cw), BF16),
            pltpu.VMEM((rows, cw), BF16),
            pltpu.VMEM((rows, cw), BF16),
            pltpu.VMEM((nb, rows, cw), F32),
            dma((4 + LOADS,)),
            dma((3, LOADS)),
            dma((heads // 2,)),
            dma((chunks,)),
            dma((reach // 2 + 1, PIECES)),
            dma((reach // 2 + 1, PIECES)),
            dma((reach + 1, PIECES)),
            dma((chunks, nb)),
            dma((chunks, nb)),
            dma((chunks, nb - 1)),
            dma((chunks, nb - 1)),
        ],
        compiler_params=pltpu.CompilerParams(
            collective_id=0, has_side_effects=True, vmem_limit_bytes=64 * 2**20
        ),
        cost_estimate=pl.CostEstimate(
            flops=2 * macs,
            bytes_accessed=2 * (tokens.size + w_query.size + w_out.size + 2 * width * HD),
            transcendentals=rows * heads * rows * (reach + 1),
        ),
        name="attention_layer",
    )(
        doc_lengths, tokens, w_query, w_key, w_value, w_out,
        query_gain.reshape(1, HD), key_gain.reshape(1, HD), jnp.asarray(turns_per_token()),
    )
    return (mine + jnp.sum(others.astype(F32), axis=0)).astype(BF16)


def solution(mesh):
    return jax.shard_map(
        functools.partial(local, mesh.shape["ctx"], mesh.shape["tp"]),
        mesh=mesh,
        in_specs=(P("ctx", None), P(None, "tp"), P(), P(), P("tp", None), P(), P(), P()),
        out_specs=P("ctx", "tp"),
        check_vma=False,
    )
```

```python
import functools
import math

import jax
import jax.numpy as jnp
import numpy as np
from jax import lax
from jax.experimental import pallas as pl
from jax.experimental.pallas import tpu as pltpu
from jax.sharding import PartitionSpec as P

H = 32
KVH = 4
HD = 128
EPSILON = 1e-06
ROPE_BASE = 1000000.0
HIDE = 256.0
CHUNKS = 4
PIECES = 2
LOADS = 4
MESH = pl.DeviceIdType.MESH
BF16 = jnp.bfloat16
F32 = jnp.float32


def turns_per_token():
    half = HD // 2
    freq = ROPE_BASE ** (-2.0 * np.arange(half) / HD) / (2 * math.pi)
    return np.concatenate([freq, freq])[None, :].astype(np.float32)


def cos_of_turns(turns):
    x = (turns - jnp.round(turns)) * (2 * math.pi)
    x2 = x * x
    out = jnp.full_like(x2, 1.0 / math.factorial(16))
    for n in range(14, -1, -2):
        out = out * x2 + (-1.0) ** (n // 2) / math.factorial(n)
    return out


def mm(a, b):
    return jnp.dot(a, b, preferred_element_type=F32)


def norm_rotate(u, gain, cos2, sin2):
    inv = lax.rsqrt(jnp.mean(u * u, axis=-1, keepdims=True) + EPSILON)
    w = u * inv * gain
    return w * cos2 + pltpu.roll(w, HD // 2, 1) * sin2


def kernel(
    reach, n_ctx, n_tp, docs,
    docs_hbm, tok_hbm, wq_hbm, wk_hbm, wv_hbm, wo_hbm, qg_hbm, kg_hbm, fr_hbm,
    mine_ref, r2,
    docs_ref, tok, wkv, wq, wo, qg, kg, fr, cos2, sin2, kv, kt, vt, q_s, acc, att, s1, r1, s2, s1_own, r1_own, own,
    in_sem, tok_sem, wq_sem, own_sem, z_send, y_send, kv_recv, s1_send, s1_recv, s2_send, s2_recv,
):
    rows = tok.shape[0]
    heads = wq.shape[1] // HD
    wide = kt.shape[1] - HD
    chunks, qrows, _ = q_s.shape
    ct = rows // chunks
    nb = n_tp // 2
    cw = mine_ref.shape[1]
    i = lax.axis_index("ctx")
    t = lax.axis_index("tp")
    pair = i + 1 - 2 * (i % 2)
    odd = i % 2 == 1
    partner = t + 1 - 2 * (t % 2)
    kv_head = t * heads // (H // KVH)

    def fetch(src, dst, sem):
        copy = pltpu.make_async_copy(src, dst, sem)
        copy.start()
        return copy

    kv_cols = pl.ds(pl.multiple_of(kv_head * HD, HD), HD)
    small = [
        fetch(docs_hbm, docs_ref, in_sem.at[0]),
        fetch(fr_hbm, fr, in_sem.at[1]),
        fetch(qg_hbm, qg, in_sem.at[2]),
        fetch(kg_hbm, kg, in_sem.at[3]),
    ]
    first = []
    for n in range(LOADS):
        some = pl.ds(n * (rows // LOADS), rows // LOADS)
        first.append(fetch(tok_hbm.at[some], tok.at[some], tok_sem.at[0, n]))
        deep = pl.ds(n * (wkv.shape[0] // LOADS), wkv.shape[0] // LOADS)
        first.append(fetch(wk_hbm.at[deep, kv_cols], wkv.at[deep, pl.ds(0, HD)], tok_sem.at[1, n]))
        first.append(fetch(wv_hbm.at[deep, kv_cols], wkv.at[deep, pl.ds(HD, HD)], tok_sem.at[2, n]))
    q_parts = heads // 2

    def wq_copy(n):
        cols = pl.ds(pl.multiple_of(n * 2 * HD, 2 * HD), 2 * HD)
        return pltpu.make_async_copy(wq_hbm.at[:, cols], wq.at[:, cols], wq_sem.at[n])

    barrier = pltpu.get_barrier_semaphore()

    def greet(where):
        pl.semaphore_signal(barrier, inc=1, device_id=where, device_id_type=MESH)

    greet((pair, t))
    greet((i, partner))
    for step in range(1, nb):
        greet((i, (t + 2 * step) % n_tp))

    @pl.when(i >= 2)
    def _():
        greet((i - 2, t))

    @pl.when(i + 2 < n_ctx)
    def _():
        greet((i + 2, t))

    lane = lax.broadcasted_iota(jnp.int32, (1, wide), 1)

    small[0].wait()

    def add_doc(d, state):
        begin, starts, ends = state
        end = begin + docs_ref[d]
        starts = jnp.where(lane == d, begin, starts)
        ends = jnp.where(lane == d, end, ends)
        return end, starts, ends

    nothing = jnp.full((1, wide), -1, jnp.int32)
    _, starts, ends = lax.fori_loop(0, docs, add_doc, (jnp.int32(0), nothing, nothing))
    local = lax.broadcasted_iota(jnp.int32, (rows, wide), 0)
    lanes = lax.broadcasted_iota(jnp.int32, (rows, wide), 1)

    def nth(j):
        if j == 0:
            return 0
        return j + (1 - i % 2) * (1 if j % 2 else -1)

    def members(d):
        pos = local + (i - d) * rows
        return (pos >= starts) & (pos < ends)

    mine = members(0)
    start = jnp.sum(jnp.where(mine, starts, 0).astype(F32), axis=1, keepdims=True)
    pos = (lax.broadcasted_iota(jnp.int32, (rows, HD), 0) + i * rows).astype(F32)
    for copy in small[1:]:
        copy.wait()
    turns = (pos - start) * fr[...]
    low = lax.broadcasted_iota(jnp.int32, (rows, HD), 1) < HD // 2
    cos2[...] = cos_of_turns(turns)
    sine = cos_of_turns(turns - 0.25)
    sin2[...] = jnp.where(low, -sine, sine)

    for copy in first:
        copy.wait()
    for n in range(q_parts):
        wq_copy(n).start()
    projected = mm(tok[...], wkv[...])
    kv[0, 0] = norm_rotate(projected[:, :HD], kg[...], cos2[...], sin2[...]).astype(BF16)
    kv[0, 1] = projected[:, HD:].astype(BF16)

    greeted = 1 + nb + jnp.where(i >= 2, 1, 0) + jnp.where(i + 2 < n_ctx, 1, 0)
    pl.semaphore_wait(barrier, greeted)

    part = rows // PIECES

    def hop(src, dst, piece, where, sems):
        here = (slice(None), pl.ds(pl.multiple_of(piece * part, part), part), slice(None))
        return pltpu.make_async_remote_copy(
            src_ref=kv.at[(src,) + here],
            dst_ref=kv.at[(dst,) + here],
            send_sem=sems.at[src // 2, piece],
            recv_sem=kv_recv.at[dst, piece],
            device_id=(where, t),
            device_id_type=MESH,
        )

    def hops(d, piece):
        there = i >= d
        moves = []
        if d + 2 <= reach:
            moves.append((there & (i + 2 < n_ctx), hop(d, d + 2, piece, i + 2, z_send)))
        if d + 1 <= reach:
            moves.append((there & jnp.logical_not(odd), hop(d, d + 1, piece, pair, y_send)))
        if d >= 2:
            moves.append((there & odd, hop(d, d - 1, piece, pair, y_send)))
        return moves

    def forward(d, pieces):
        for piece in pieces:
            if d:
                arrive(d, piece)
            for cond, copy in hops(d, piece):

                @pl.when(cond)
                def _():
                    copy.start()

    def arrive(d, piece):
        @pl.when(i >= d)
        def _():
            hop(0, d, piece, pair, z_send).wait_recv()

    every = range(PIECES)
    forward(0, every)
    deep = heads * HD // LOADS
    wo_copies = [
        fetch(
            wo_hbm.at[pl.ds(n * deep, deep)], wo.at[pl.ds(n * deep, deep)], in_sem.at[4 + n]
        )
        for n in range(LOADS)
    ]

    for d in range(reach + 1):
        vt[d, :, pl.ds(HD, HD)] = jnp.ones((rows, HD), BF16)
        held = jnp.where(members(nth(d)), HIDE, jnp.where(lanes == docs, -HIDE, 0.0))
        kt[d, pl.ds(HD, wide), :] = held.T.astype(BF16)
    q_code = jnp.where(mine | (lanes == docs), 1.0, 0.0).astype(BF16)
    for c in range(chunks):
        for h in range(heads):
            q_s[c, pl.ds(h * ct, ct), pl.ds(HD, wide)] = q_code[c * ct : (c + 1) * ct]
    for d in range(1, reach + 1):

        @pl.when(i < d)
        def _():
            kv[d] = jnp.zeros(kv.shape[1:], BF16)

    scale = HD ** (-0.5) * math.log2(math.e)

    def project(n, _):
        cols = pl.ds(pl.multiple_of(n * 2 * HD, 2 * HD), 2 * HD)
        both = mm(tok[...], wq[:, cols])
        for k in range(2):
            one = norm_rotate(both[:, k * HD : (k + 1) * HD], qg[...] * scale, cos2[...], sin2[...])
            one = one.astype(BF16)
            at = pl.multiple_of((n * 2 + k) * ct, ct)
            for c in range(chunks):
                q_s[c, pl.ds(at, ct), pl.ds(0, HD)] = one[c * ct : (c + 1) * ct]
        return 0

    def query_part(n, _):
        wq_copy(n).wait()
        project(n, 0)

        @pl.when(n >= q_parts - PIECES + 1)
        def _():
            forward(2, [n - (q_parts - PIECES + 1)])

        return 0

    lax.fori_loop(0, q_parts, query_part, 0)
    forward(2, every[PIECES - 1 :])

    group = min(8, heads)
    grows = group * ct
    groups = heads // group

    def weights_of(c, at, j):
        weights = jnp.exp2(mm(q_s[c, pl.ds(at, grows), :], kt[j]))
        if j == 0:
            token = lax.broadcasted_iota(jnp.int32, (ct, rows), 0) + c * ct
            seen = lax.broadcasted_iota(jnp.int32, (ct, rows), 1) <= token
            weights = jnp.where(seen[None], weights.reshape(group, ct, rows), 0.0)
            weights = weights.reshape(grows, rows)
        return weights.astype(BF16)

    def weighted(c, at, slots):
        weights = jnp.concatenate([weights_of(c, at, j) for j in slots], axis=1)
        return mm(weights, jnp.concatenate([vt[j] for j in slots], axis=0))

    def place(j, d):
        if d % 2:

            @pl.when(i >= d)
            def _():
                for piece in every:
                    hop(0, d, piece, pair, z_send).wait_recv()

        kt[j, pl.ds(0, HD), :] = kv[d, 0].astype(F32).T.astype(BF16)
        vt[j, :, pl.ds(0, HD)] = kv[d, 1]

    def turn(j):
        if j == 0:
            place(0, 0)
            return

        @pl.when(odd)
        def _():
            place(j, j)

        @pl.when(jnp.logical_not(odd))
        def _():
            place(j, j + 1 if j % 2 else j - 1)

    def attend(slots):
        for j in slots:
            turn(j)

        def step(n, _):
            c = n // groups
            at = pl.multiple_of((n % groups) * grows, grows)
            new = weighted(c, at, slots)
            if slots[0] == 0:
                acc[c, pl.ds(at, grows), :] = new
            else:
                acc[c, pl.ds(at, grows), :] += new
            return 0

        lax.fori_loop(0, chunks * groups, step, 0)

    forward(4, every[:1])
    attend((0, 1))
    forward(4, every[1:])
    for j in range(2, reach, 2):
        if j > 2:
            forward(j + 2, every)
        attend((j, j + 1))
    turn(reach)

    for copy in wo_copies:
        copy.wait()

    def some_rows(c):
        return pl.ds(pl.multiple_of(c * ct, ct), ct)

    def pair_copy(c, k):
        return pltpu.make_async_remote_copy(
            src_ref=s1.at[c, k - 1],
            dst_ref=r1.at[c, k - 1],
            send_sem=s1_send.at[c, k],
            recv_sem=s1_recv.at[c, k],
            device_id=(i, partner),
            device_id_type=MESH,
        )

    def chip_copy(c, k):
        return pltpu.make_async_remote_copy(
            src_ref=s2.at[c, k - 1],
            dst_ref=r2.at[k - 1, some_rows(c)],
            send_sem=s2_send.at[c, k - 1],
            recv_sem=s2_recv.at[c, k - 1],
            device_id=(i, (t + 2 * k) % n_tp),
            device_id_type=MESH,
        )

    own_copy = pltpu.make_async_remote_copy(
        src_ref=s1_own,
        dst_ref=r1_own,
        send_sem=s1_send.at[0, 0],
        recv_sem=s1_recv.at[0, 0],
        device_id=(i, partner),
        device_id_type=MESH,
    )
    kept = pltpu.make_async_copy(own.at[0], mine_ref, own_sem.at[0])

    def columns(owner):
        return pl.ds(pl.multiple_of(owner * cw, cw), cw)

    def finish(c):
        def step(n, _):
            at = pl.multiple_of(n * grows, grows)
            total = acc[c, pl.ds(at, grows), :] + weighted(c, at, (reach,))
            done = (total[:, :HD] / total[:, HD:]).astype(BF16)
            for h in range(group):
                cols = pl.ds(pl.multiple_of(n * group * HD + h * HD, HD), HD)
                att[some_rows(c), cols] = done[h * ct : (h + 1) * ct]
            return 0

        if groups == 1:
            step(0, 0)
        else:
            lax.fori_loop(0, groups, step, 0)

    def pair_sum(c):
        for k in range(1, nb):
            pair_copy(c, k).wait_recv()
            term = own[k, some_rows(c)] + r1[c, k - 1].astype(F32)
            s2[c, k - 1] = term.astype(BF16)
            chip_copy(c, k).start()

    def chunk(c, _):
        finish(c)

        @pl.when(c >= 1)
        def _():
            pair_sum(c - 1)

        for k in range(1, nb):
            term = mm(att[some_rows(c)], wo[:, columns((partner + 2 * k) % n_tp)])
            s1[c, k - 1] = term.astype(BF16)
            pair_copy(c, k).start()
        for k in range(1, nb):
            term = mm(att[some_rows(c)], wo[:, columns((t + 2 * k) % n_tp)])
            own[k, some_rows(c)] = term.astype(BF16).astype(F32)
        return 0

    lax.fori_loop(0, chunks, chunk, 0)
    pair_sum(chunks - 1)
    s1_own[...] = mm(att[...], wo[:, columns(partner)]).astype(BF16)
    own_copy.start()
    own[0] = mm(att[...], wo[:, columns(t)]).astype(BF16).astype(F32)
    own_copy.wait_recv()
    own[0] += r1_own[...].astype(F32)
    kept.start()
    own_copy.wait_send()
    kept.wait()
    for c in range(chunks):
        for k in range(1, nb):
            pair_copy(c, k).wait_send()
            chip_copy(c, k).wait_send()
    for d in range(0, reach + 1, 2):
        for piece in every:
            for cond, copy in hops(d, piece):

                @pl.when(cond)
                def _():
                    copy.wait_send()
    for c in range(chunks):
        for k in range(1, nb):
            chip_copy(c, k).wait_recv()


def local(n_ctx, n_tp, tokens, w_query, w_key, w_value, w_out, query_gain, key_gain, doc_lengths):
    rows, width = tokens.shape
    heads = w_query.shape[1] // HD
    out_width = w_out.shape[1]
    reach = min(16, n_ctx // 2)
    docs = doc_lengths.shape[0]
    wide = -(-(docs + 1) // 128) * 128
    chunks = CHUNKS
    ct = rows // chunks
    nb = n_tp // 2
    cw = out_width // n_tp
    dma = pltpu.SemaphoreType.DMA
    anywhere = pl.BlockSpec(memory_space=pltpu.HBM)
    macs = rows * width * (heads + 2) * HD + rows * heads * HD * out_width
    macs += 2 * rows * heads * rows * (reach + 1) * 2 * HD
    mine, others = pl.pallas_call(
        functools.partial(kernel, reach, n_ctx, n_tp, docs),
        out_shape=(
            jax.ShapeDtypeStruct((rows, cw), F32),
            jax.ShapeDtypeStruct((nb - 1, rows, cw), BF16),
        ),
        in_specs=[anywhere] * 9,
        out_specs=(anywhere, anywhere),
        scratch_shapes=[
            pltpu.SMEM((docs,), jnp.int32),
            pltpu.VMEM((rows, width), BF16),
            pltpu.VMEM((width, 2 * HD), BF16),
            pltpu.VMEM((width, heads * HD), BF16),
            pltpu.VMEM((heads * HD, out_width), BF16),
            pltpu.VMEM((1, HD), F32),
            pltpu.VMEM((1, HD), F32),
            pltpu.VMEM((1, HD), F32),
            pltpu.VMEM((rows, HD), F32),
            pltpu.VMEM((rows, HD), F32),
            pltpu.VMEM((reach + 1, 2, rows, HD), BF16),
            pltpu.VMEM((reach + 1, HD + wide, rows), BF16),
            pltpu.VMEM((reach + 1, rows, 2 * HD), BF16),
            pltpu.VMEM((chunks, heads * ct, HD + wide), BF16),
            pltpu.VMEM((chunks, heads * ct, 2 * HD), F32),
            pltpu.VMEM((rows, heads * HD), BF16),
            pltpu.VMEM((chunks, nb - 1, ct, cw), BF16),
            pltpu.VMEM((chunks, nb - 1, ct, cw), BF16),
            pltpu.VMEM((chunks, nb - 1, ct, cw), BF16),
            pltpu.VMEM((rows, cw), BF16),
            pltpu.VMEM((rows, cw), BF16),
            pltpu.VMEM((nb, rows, cw), F32),
            dma((4 + LOADS,)),
            dma((3, LOADS)),
            dma((heads // 2,)),
            dma((chunks,)),
            dma((reach // 2 + 1, PIECES)),
            dma((reach // 2 + 1, PIECES)),
            dma((reach + 1, PIECES)),
            dma((chunks, nb)),
            dma((chunks, nb)),
            dma((chunks, nb - 1)),
            dma((chunks, nb - 1)),
        ],
        compiler_params=pltpu.CompilerParams(
            collective_id=0, has_side_effects=True, vmem_limit_bytes=64 * 2**20
        ),
        cost_estimate=pl.CostEstimate(
            flops=2 * macs,
            bytes_accessed=2 * (tokens.size + w_query.size + w_out.size + 2 * width * HD),
            transcendentals=rows * heads * rows * (reach + 1),
        ),
        name="attention_layer",
    )(
        doc_lengths, tokens, w_query, w_key, w_value, w_out,
        query_gain.reshape(1, HD), key_gain.reshape(1, HD), jnp.asarray(turns_per_token()),
    )
    return (mine + jnp.sum(others.astype(F32), axis=0)).astype(BF16)


def solution(mesh):
    return jax.shard_map(
        functools.partial(local, mesh.shape["ctx"], mesh.shape["tp"]),
        mesh=mesh,
        in_specs=(P("ctx", None), P(None, "tp"), P(), P(), P("tp", None), P(), P(), P()),
        out_specs=P("ctx", "tp"),
        check_vma=False,
    )
```

```python
import functools
import math

import jax
import jax.numpy as jnp
import numpy as np
from jax import lax
from jax.experimental import pallas as pl
from jax.experimental.pallas import tpu as pltpu
from jax.sharding import PartitionSpec as P

H = 32
KVH = 4
HD = 128
EPSILON = 1e-06
ROPE_BASE = 1000000.0
HIDE = 256.0
CHUNKS = 4
PIECES = 4
LOADS = 4
MESH = pl.DeviceIdType.MESH
BF16 = jnp.bfloat16
F32 = jnp.float32


def turns_per_token():
    half = HD // 2
    freq = ROPE_BASE ** (-2.0 * np.arange(half) / HD) / (2 * math.pi)
    return np.concatenate([freq, freq])[None, :].astype(np.float32)


def cos_of_turns(turns):
    x = (turns - jnp.round(turns)) * (2 * math.pi)
    x2 = x * x
    out = jnp.full_like(x2, 1.0 / math.factorial(16))
    for n in range(14, -1, -2):
        out = out * x2 + (-1.0) ** (n // 2) / math.factorial(n)
    return out


def mm(a, b):
    return jnp.dot(a, b, preferred_element_type=F32)


def norm_rotate(u, gain, cos2, sin2):
    inv = lax.rsqrt(jnp.mean(u * u, axis=-1, keepdims=True) + EPSILON)
    w = u * inv * gain
    return w * cos2 + pltpu.roll(w, HD // 2, 1) * sin2


def kernel(
    reach, n_ctx, n_tp, docs,
    docs_hbm, tok_hbm, wq_hbm, wk_hbm, wv_hbm, wo_hbm, qg_hbm, kg_hbm, fr_hbm,
    mine_ref, r2,
    docs_ref, tok, wkv, wq, wo, qg, kg, fr, cos2, sin2, kv, kt, vt, q_s, acc, att, s1, r1, s2, s1_own, r1_own, own,
    in_sem, tok_sem, wq_sem, own_sem, z_send, y_send, kv_recv, s1_send, s1_recv, s2_send, s2_recv,
):
    rows = tok.shape[0]
    heads = wq.shape[1] // HD
    wide = kt.shape[1] - HD
    chunks, qrows, _ = q_s.shape
    ct = rows // chunks
    nb = n_tp // 2
    cw = mine_ref.shape[1]
    i = lax.axis_index("ctx")
    t = lax.axis_index("tp")
    pair = i + 1 - 2 * (i % 2)
    odd = i % 2 == 1
    partner = t + 1 - 2 * (t % 2)
    kv_head = t * heads // (H // KVH)

    def fetch(src, dst, sem):
        copy = pltpu.make_async_copy(src, dst, sem)
        copy.start()
        return copy

    kv_cols = pl.ds(pl.multiple_of(kv_head * HD, HD), HD)
    small = [
        fetch(docs_hbm, docs_ref, in_sem.at[0]),
        fetch(fr_hbm, fr, in_sem.at[1]),
        fetch(qg_hbm, qg, in_sem.at[2]),
        fetch(kg_hbm, kg, in_sem.at[3]),
    ]
    first = []
    for n in range(LOADS):
        some = pl.ds(n * (rows // LOADS), rows // LOADS)
        first.append(fetch(tok_hbm.at[some], tok.at[some], tok_sem.at[0, n]))
        deep = pl.ds(n * (wkv.shape[0] // LOADS), wkv.shape[0] // LOADS)
        first.append(fetch(wk_hbm.at[deep, kv_cols], wkv.at[deep, pl.ds(0, HD)], tok_sem.at[1, n]))
        first.append(fetch(wv_hbm.at[deep, kv_cols], wkv.at[deep, pl.ds(HD, HD)], tok_sem.at[2, n]))
    q_parts = heads // 2

    def wq_copy(n):
        cols = pl.ds(pl.multiple_of(n * 2 * HD, 2 * HD), 2 * HD)
        return pltpu.make_async_copy(wq_hbm.at[:, cols], wq.at[:, cols], wq_sem.at[n])

    barrier = pltpu.get_barrier_semaphore()

    def greet(where):
        pl.semaphore_signal(barrier, inc=1, device_id=where, device_id_type=MESH)

    greet((pair, t))
    greet((i, partner))
    for step in range(1, nb):
        greet((i, (t + 2 * step) % n_tp))

    @pl.when(i >= 2)
    def _():
        greet((i - 2, t))

    @pl.when(i + 2 < n_ctx)
    def _():
        greet((i + 2, t))

    lane = lax.broadcasted_iota(jnp.int32, (1, wide), 1)

    small[0].wait()

    def add_doc(d, state):
        begin, starts, ends = state
        end = begin + docs_ref[d]
        starts = jnp.where(lane == d, begin, starts)
        ends = jnp.where(lane == d, end, ends)
        return end, starts, ends

    nothing = jnp.full((1, wide), -1, jnp.int32)
    _, starts, ends = lax.fori_loop(0, docs, add_doc, (jnp.int32(0), nothing, nothing))
    local = lax.broadcasted_iota(jnp.int32, (rows, wide), 0)
    lanes = lax.broadcasted_iota(jnp.int32, (rows, wide), 1)

    def nth(j):
        if j == 0:
            return 0
        return j + (1 - i % 2) * (1 if j % 2 else -1)

    def members(d):
        pos = local + (i - d) * rows
        return (pos >= starts) & (pos < ends)

    mine = members(0)
    start = jnp.sum(jnp.where(mine, starts, 0).astype(F32), axis=1, keepdims=True)
    pos = (lax.broadcasted_iota(jnp.int32, (rows, HD), 0) + i * rows).astype(F32)
    for copy in small[1:]:
        copy.wait()
    turns = (pos - start) * fr[...]
    low = lax.broadcasted_iota(jnp.int32, (rows, HD), 1) < HD // 2
    cos2[...] = cos_of_turns(turns)
    sine = cos_of_turns(turns - 0.25)
    sin2[...] = jnp.where(low, -sine, sine)

    for copy in first:
        copy.wait()
    for n in range(q_parts):
        wq_copy(n).start()
    projected = mm(tok[...], wkv[...])
    kv[0, 0] = norm_rotate(projected[:, :HD], kg[...], cos2[...], sin2[...]).astype(BF16)
    kv[0, 1] = projected[:, HD:].astype(BF16)

    greeted = 1 + nb + jnp.where(i >= 2, 1, 0) + jnp.where(i + 2 < n_ctx, 1, 0)
    pl.semaphore_wait(barrier, greeted)

    part = rows // PIECES

    def hop(src, dst, piece, where, sems):
        here = (slice(None), pl.ds(pl.multiple_of(piece * part, part), part), slice(None))
        return pltpu.make_async_remote_copy(
            src_ref=kv.at[(src,) + here],
            dst_ref=kv.at[(dst,) + here],
            send_sem=sems.at[src // 2, piece],
            recv_sem=kv_recv.at[dst, piece],
            device_id=(where, t),
            device_id_type=MESH,
        )

    def hops(d, piece):
        there = i >= d
        moves = []
        if d + 2 <= reach:
            moves.append((there & (i + 2 < n_ctx), hop(d, d + 2, piece, i + 2, z_send)))
        if d + 1 <= reach:
            moves.append((there & jnp.logical_not(odd), hop(d, d + 1, piece, pair, y_send)))
        if d >= 2:
            moves.append((there & odd, hop(d, d - 1, piece, pair, y_send)))
        return moves

    def forward(d, pieces):
        for piece in pieces:
            if d:
                arrive(d, piece)
            for cond, copy in hops(d, piece):

                @pl.when(cond)
                def _():
                    copy.start()

    def arrive(d, piece):
        @pl.when(i >= d)
        def _():
            hop(0, d, piece, pair, z_send).wait_recv()

    every = range(PIECES)
    forward(0, every)
    deep = heads * HD // LOADS
    wo_copies = [
        fetch(
            wo_hbm.at[pl.ds(n * deep, deep)], wo.at[pl.ds(n * deep, deep)], in_sem.at[4 + n]
        )
        for n in range(LOADS)
    ]

    for d in range(reach + 1):
        vt[d, :, pl.ds(HD, HD)] = jnp.ones((rows, HD), BF16)
        held = jnp.where(members(nth(d)), HIDE, jnp.where(lanes == docs, -HIDE, 0.0))
        kt[d, pl.ds(HD, wide), :] = held.T.astype(BF16)
    q_code = jnp.where(mine | (lanes == docs), 1.0, 0.0).astype(BF16)
    for c in range(chunks):
        for h in range(heads):
            q_s[c, pl.ds(h * ct, ct), pl.ds(HD, wide)] = q_code[c * ct : (c + 1) * ct]
    for d in range(1, reach + 1):

        @pl.when(i < d)
        def _():
            kv[d] = jnp.zeros(kv.shape[1:], BF16)

    scale = HD ** (-0.5) * math.log2(math.e)

    def project(n, _):
        cols = pl.ds(pl.multiple_of(n * 2 * HD, 2 * HD), 2 * HD)
        both = mm(tok[...], wq[:, cols])
        for k in range(2):
            one = norm_rotate(both[:, k * HD : (k + 1) * HD], qg[...] * scale, cos2[...], sin2[...])
            one = one.astype(BF16)
            at = pl.multiple_of((n * 2 + k) * ct, ct)
            for c in range(chunks):
                q_s[c, pl.ds(at, ct), pl.ds(0, HD)] = one[c * ct : (c + 1) * ct]
        return 0

    def query_part(n, _):
        wq_copy(n).wait()
        project(n, 0)

        @pl.when(n >= 1)
        def _():
            forward(2, [n - 1])

        return 0

    lax.fori_loop(0, q_parts, query_part, 0)
    forward(2, every[q_parts - 1 :])

    group = min(8, heads)
    grows = group * ct
    groups = heads // group

    def weights_of(c, at, j):
        weights = jnp.exp2(mm(q_s[c, pl.ds(at, grows), :], kt[j]))
        if j == 0:
            token = lax.broadcasted_iota(jnp.int32, (ct, rows), 0) + c * ct
            seen = lax.broadcasted_iota(jnp.int32, (ct, rows), 1) <= token
            weights = jnp.where(seen[None], weights.reshape(group, ct, rows), 0.0)
            weights = weights.reshape(grows, rows)
        return weights.astype(BF16)

    def weighted(c, at, slots):
        weights = jnp.concatenate([weights_of(c, at, j) for j in slots], axis=1)
        return mm(weights, jnp.concatenate([vt[j] for j in slots], axis=0))

    def place(j, d):
        if d % 2:

            @pl.when(i >= d)
            def _():
                for piece in every:
                    hop(0, d, piece, pair, z_send).wait_recv()

        kt[j, pl.ds(0, HD), :] = kv[d, 0].astype(F32).T.astype(BF16)
        vt[j, :, pl.ds(0, HD)] = kv[d, 1]

    def turn(j):
        if j == 0:
            place(0, 0)
            return

        @pl.when(odd)
        def _():
            place(j, j)

        @pl.when(jnp.logical_not(odd))
        def _():
            place(j, j + 1 if j % 2 else j - 1)

    def attend(slots, between=None):
        for j in slots:
            turn(j)

        def step(n, _):
            c = n // groups
            at = pl.multiple_of((n % groups) * grows, grows)
            new = weighted(c, at, slots)
            if slots[0] == 0:
                acc[c, pl.ds(at, grows), :] = new
            else:
                acc[c, pl.ds(at, grows), :] += new
            if between is not None:
                between(n)
            return 0

        lax.fori_loop(0, chunks * groups, step, 0)

    steps = chunks * groups

    def second_hop(n):
        @pl.when(n < PIECES)
        def _():
            forward(4, [n])

    attend((0, 1), second_hop)
    forward(4, every[steps:])
    for j in range(2, reach, 2):
        if j > 2:
            forward(j + 2, every)
        attend((j, j + 1))
    turn(reach)

    for copy in wo_copies:
        copy.wait()

    def some_rows(c):
        return pl.ds(pl.multiple_of(c * ct, ct), ct)

    def pair_copy(c, k):
        return pltpu.make_async_remote_copy(
            src_ref=s1.at[c, k - 1],
            dst_ref=r1.at[c, k - 1],
            send_sem=s1_send.at[c, k],
            recv_sem=s1_recv.at[c, k],
            device_id=(i, partner),
            device_id_type=MESH,
        )

    def chip_copy(c, k):
        return pltpu.make_async_remote_copy(
            src_ref=s2.at[c, k - 1],
            dst_ref=r2.at[k - 1, some_rows(c)],
            send_sem=s2_send.at[c, k - 1],
            recv_sem=s2_recv.at[c, k - 1],
            device_id=(i, (t + 2 * k) % n_tp),
            device_id_type=MESH,
        )

    own_copy = pltpu.make_async_remote_copy(
        src_ref=s1_own,
        dst_ref=r1_own,
        send_sem=s1_send.at[0, 0],
        recv_sem=s1_recv.at[0, 0],
        device_id=(i, partner),
        device_id_type=MESH,
    )
    kept = pltpu.make_async_copy(own.at[0], mine_ref, own_sem.at[0])

    def columns(owner):
        return pl.ds(pl.multiple_of(owner * cw, cw), cw)

    def finish(c):
        def step(n, _):
            at = pl.multiple_of(n * grows, grows)
            total = acc[c, pl.ds(at, grows), :] + weighted(c, at, (reach,))
            done = (total[:, :HD] / total[:, HD:]).astype(BF16)
            for h in range(group):
                cols = pl.ds(pl.multiple_of(n * group * HD + h * HD, HD), HD)
                att[some_rows(c), cols] = done[h * ct : (h + 1) * ct]
            return 0

        if groups == 1:
            step(0, 0)
        else:
            lax.fori_loop(0, groups, step, 0)

    def pair_sum(c):
        for k in range(1, nb):
            pair_copy(c, k).wait_recv()
            term = own[k, some_rows(c)] + r1[c, k - 1].astype(F32)
            s2[c, k - 1] = term.astype(BF16)
            chip_copy(c, k).start()

    def chunk(c, _):
        finish(c)

        @pl.when(c >= 1)
        def _():
            pair_sum(c - 1)

        for k in range(1, nb):
            term = mm(att[some_rows(c)], wo[:, columns((partner + 2 * k) % n_tp)])
            s1[c, k - 1] = term.astype(BF16)
            pair_copy(c, k).start()
        for k in range(1, nb):
            term = mm(att[some_rows(c)], wo[:, columns((t + 2 * k) % n_tp)])
            own[k, some_rows(c)] = term.astype(BF16).astype(F32)
        return 0

    lax.fori_loop(0, chunks, chunk, 0)
    pair_sum(chunks - 1)
    s1_own[...] = mm(att[...], wo[:, columns(partner)]).astype(BF16)
    own_copy.start()
    own[0] = mm(att[...], wo[:, columns(t)]).astype(BF16).astype(F32)
    own_copy.wait_recv()
    own[0] += r1_own[...].astype(F32)
    kept.start()
    own_copy.wait_send()
    kept.wait()
    for c in range(chunks):
        for k in range(1, nb):
            pair_copy(c, k).wait_send()
            chip_copy(c, k).wait_send()
    for d in range(0, reach + 1, 2):
        for piece in every:
            for cond, copy in hops(d, piece):

                @pl.when(cond)
                def _():
                    copy.wait_send()
    for c in range(chunks):
        for k in range(1, nb):
            chip_copy(c, k).wait_recv()


def local(n_ctx, n_tp, tokens, w_query, w_key, w_value, w_out, query_gain, key_gain, doc_lengths):
    rows, width = tokens.shape
    heads = w_query.shape[1] // HD
    out_width = w_out.shape[1]
    reach = min(16, n_ctx // 2)
    docs = doc_lengths.shape[0]
    wide = -(-(docs + 1) // 128) * 128
    chunks = CHUNKS
    ct = rows // chunks
    nb = n_tp // 2
    cw = out_width // n_tp
    dma = pltpu.SemaphoreType.DMA
    anywhere = pl.BlockSpec(memory_space=pltpu.HBM)
    macs = rows * width * (heads + 2) * HD + rows * heads * HD * out_width
    macs += 2 * rows * heads * rows * (reach + 1) * 2 * HD
    mine, others = pl.pallas_call(
        functools.partial(kernel, reach, n_ctx, n_tp, docs),
        out_shape=(
            jax.ShapeDtypeStruct((rows, cw), F32),
            jax.ShapeDtypeStruct((nb - 1, rows, cw), BF16),
        ),
        in_specs=[anywhere] * 9,
        out_specs=(anywhere, anywhere),
        scratch_shapes=[
            pltpu.SMEM((docs,), jnp.int32),
            pltpu.VMEM((rows, width), BF16),
            pltpu.VMEM((width, 2 * HD), BF16),
            pltpu.VMEM((width, heads * HD), BF16),
            pltpu.VMEM((heads * HD, out_width), BF16),
            pltpu.VMEM((1, HD), F32),
            pltpu.VMEM((1, HD), F32),
            pltpu.VMEM((1, HD), F32),
            pltpu.VMEM((rows, HD), F32),
            pltpu.VMEM((rows, HD), F32),
            pltpu.VMEM((reach + 1, 2, rows, HD), BF16),
            pltpu.VMEM((reach + 1, HD + wide, rows), BF16),
            pltpu.VMEM((reach + 1, rows, 2 * HD), BF16),
            pltpu.VMEM((chunks, heads * ct, HD + wide), BF16),
            pltpu.VMEM((chunks, heads * ct, 2 * HD), F32),
            pltpu.VMEM((rows, heads * HD), BF16),
            pltpu.VMEM((chunks, nb - 1, ct, cw), BF16),
            pltpu.VMEM((chunks, nb - 1, ct, cw), BF16),
            pltpu.VMEM((chunks, nb - 1, ct, cw), BF16),
            pltpu.VMEM((rows, cw), BF16),
            pltpu.VMEM((rows, cw), BF16),
            pltpu.VMEM((nb, rows, cw), F32),
            dma((4 + LOADS,)),
            dma((3, LOADS)),
            dma((heads // 2,)),
            dma((chunks,)),
            dma((reach // 2 + 1, PIECES)),
            dma((reach // 2 + 1, PIECES)),
            dma((reach + 1, PIECES)),
            dma((chunks, nb)),
            dma((chunks, nb)),
            dma((chunks, nb - 1)),
            dma((chunks, nb - 1)),
        ],
        compiler_params=pltpu.CompilerParams(
            collective_id=0, has_side_effects=True, vmem_limit_bytes=64 * 2**20
        ),
        cost_estimate=pl.CostEstimate(
            flops=2 * macs,
            bytes_accessed=2 * (tokens.size + w_query.size + w_out.size + 2 * width * HD),
            transcendentals=rows * heads * rows * (reach + 1),
        ),
        name="attention_layer",
    )(
        doc_lengths, tokens, w_query, w_key, w_value, w_out,
        query_gain.reshape(1, HD), key_gain.reshape(1, HD), jnp.asarray(turns_per_token()),
    )
    return (mine + jnp.sum(others.astype(F32), axis=0)).astype(BF16)


def solution(mesh):
    return jax.shard_map(
        functools.partial(local, mesh.shape["ctx"], mesh.shape["tp"]),
        mesh=mesh,
        in_specs=(P("ctx", None), P(None, "tp"), P(), P(), P("tp", None), P(), P(), P()),
        out_specs=P("ctx", "tp"),
        check_vma=False,
    )
```

```python
import functools
import math

import jax
import jax.numpy as jnp
import numpy as np
from jax import lax
from jax.experimental import pallas as pl
from jax.experimental.pallas import tpu as pltpu
from jax.sharding import PartitionSpec as P

H = 32
KVH = 4
HD = 128
EPSILON = 1e-06
ROPE_BASE = 1000000.0
HIDE = 256.0
CHUNKS = 4
PIECES = 4
LOADS = 4
MESH = pl.DeviceIdType.MESH
BF16 = jnp.bfloat16
F32 = jnp.float32


def turns_per_token():
    half = HD // 2
    freq = ROPE_BASE ** (-2.0 * np.arange(half) / HD) / (2 * math.pi)
    return np.concatenate([freq, freq])[None, :].astype(np.float32)


def cos_of_turns(turns):
    x = (turns - jnp.round(turns)) * (2 * math.pi)
    x2 = x * x
    out = jnp.full_like(x2, 1.0 / math.factorial(16))
    for n in range(14, -1, -2):
        out = out * x2 + (-1.0) ** (n // 2) / math.factorial(n)
    return out


def mm(a, b):
    return jnp.dot(a, b, preferred_element_type=F32)


def norm_rotate(u, gain, cos2, sin2):
    inv = lax.rsqrt(jnp.mean(u * u, axis=-1, keepdims=True) + EPSILON)
    w = u * inv * gain
    return w * cos2 + pltpu.roll(w, HD // 2, 1) * sin2


def kernel(
    reach, n_ctx, n_tp, docs,
    docs_hbm, tok_hbm, wq_hbm, wk_hbm, wv_hbm, wo_hbm, qg_hbm, kg_hbm, fr_hbm,
    mine_ref, r2,
    docs_ref, tok, wkv, wq, wo, qg, kg, fr, cos2, sin2, kv, kt, vt, q_s, acc, att, s1, r1, s2, s1_own, r1_own, own,
    in_sem, tok_sem, wq_sem, own_sem, z_send, y_send, kv_recv, s1_send, s1_recv, s2_send, s2_recv,
):
    rows = tok.shape[0]
    heads = wq.shape[1] // HD
    wide = kt.shape[1] - HD
    chunks, qrows, _ = q_s.shape
    ct = rows // chunks
    nb = n_tp // 2
    cw = mine_ref.shape[1]
    i = lax.axis_index("ctx")
    t = lax.axis_index("tp")
    pair = i + 1 - 2 * (i % 2)
    odd = i % 2 == 1
    partner = t + 1 - 2 * (t % 2)
    kv_head = t * heads // (H // KVH)

    def fetch(src, dst, sem):
        copy = pltpu.make_async_copy(src, dst, sem)
        copy.start()
        return copy

    kv_cols = pl.ds(pl.multiple_of(kv_head * HD, HD), HD)
    small = [
        fetch(docs_hbm, docs_ref, in_sem.at[0]),
        fetch(fr_hbm, fr, in_sem.at[1]),
        fetch(qg_hbm, qg, in_sem.at[2]),
        fetch(kg_hbm, kg, in_sem.at[3]),
    ]
    first = []
    for n in range(LOADS):
        some = pl.ds(n * (rows // LOADS), rows // LOADS)
        first.append(fetch(tok_hbm.at[some], tok.at[some], tok_sem.at[0, n]))
        deep = pl.ds(n * (wkv.shape[0] // LOADS), wkv.shape[0] // LOADS)
        first.append(fetch(wk_hbm.at[deep, kv_cols], wkv.at[deep, pl.ds(0, HD)], tok_sem.at[1, n]))
        first.append(fetch(wv_hbm.at[deep, kv_cols], wkv.at[deep, pl.ds(HD, HD)], tok_sem.at[2, n]))
    q_parts = heads // 2

    def wq_copy(n):
        cols = pl.ds(pl.multiple_of(n * 2 * HD, 2 * HD), 2 * HD)
        return pltpu.make_async_copy(wq_hbm.at[:, cols], wq.at[:, cols], wq_sem.at[n])

    barrier = pltpu.get_barrier_semaphore()

    def greet(where):
        pl.semaphore_signal(barrier, inc=1, device_id=where, device_id_type=MESH)

    greet((pair, t))
    greet((i, partner))
    for step in range(1, nb):
        greet((i, (t + 2 * step) % n_tp))

    @pl.when(i >= 2)
    def _():
        greet((i - 2, t))

    @pl.when(i + 2 < n_ctx)
    def _():
        greet((i + 2, t))

    lane = lax.broadcasted_iota(jnp.int32, (1, wide), 1)

    small[0].wait()

    def add_doc(d, state):
        begin, starts, ends = state
        end = begin + docs_ref[d]
        starts = jnp.where(lane == d, begin, starts)
        ends = jnp.where(lane == d, end, ends)
        return end, starts, ends

    nothing = jnp.full((1, wide), -1, jnp.int32)
    _, starts, ends = lax.fori_loop(0, docs, add_doc, (jnp.int32(0), nothing, nothing))
    local = lax.broadcasted_iota(jnp.int32, (rows, wide), 0)
    lanes = lax.broadcasted_iota(jnp.int32, (rows, wide), 1)

    def nth(j):
        if j == 0:
            return 0
        return j + (1 - i % 2) * (1 if j % 2 else -1)

    def members(d):
        pos = local + (i - d) * rows
        return (pos >= starts) & (pos < ends)

    mine = members(0)
    start = jnp.sum(jnp.where(mine, starts, 0).astype(F32), axis=1, keepdims=True)
    pos = (lax.broadcasted_iota(jnp.int32, (rows, HD), 0) + i * rows).astype(F32)
    for copy in small[1:]:
        copy.wait()
    turns = (pos - start) * fr[...]
    low = lax.broadcasted_iota(jnp.int32, (rows, HD), 1) < HD // 2
    cos2[...] = cos_of_turns(turns)
    sine = cos_of_turns(turns - 0.25)
    sin2[...] = jnp.where(low, -sine, sine)

    for copy in first:
        copy.wait()
    for n in range(q_parts):
        wq_copy(n).start()
    projected = mm(tok[...], wkv[...])
    kv[0, 0] = norm_rotate(projected[:, :HD], kg[...], cos2[...], sin2[...]).astype(BF16)
    kv[0, 1] = projected[:, HD:].astype(BF16)

    greeted = 1 + nb + jnp.where(i >= 2, 1, 0) + jnp.where(i + 2 < n_ctx, 1, 0)
    pl.semaphore_wait(barrier, greeted)

    part = rows // PIECES

    def hop(src, dst, piece, where, sems):
        here = (slice(None), pl.ds(pl.multiple_of(piece * part, part), part), slice(None))
        return pltpu.make_async_remote_copy(
            src_ref=kv.at[(src,) + here],
            dst_ref=kv.at[(dst,) + here],
            send_sem=sems.at[src // 2, piece],
            recv_sem=kv_recv.at[dst, piece],
            device_id=(where, t),
            device_id_type=MESH,
        )

    def hops(d, piece):
        there = i >= d
        moves = []
        if d + 2 <= reach:
            moves.append((there & (i + 2 < n_ctx), hop(d, d + 2, piece, i + 2, z_send)))
        if d + 1 <= reach:
            moves.append((there & jnp.logical_not(odd), hop(d, d + 1, piece, pair, y_send)))
        if d >= 2:
            moves.append((there & odd, hop(d, d - 1, piece, pair, y_send)))
        return moves

    def forward(d, pieces):
        for piece in pieces:
            if d:
                arrive(d, piece)
            for cond, copy in hops(d, piece):

                @pl.when(cond)
                def _():
                    copy.start()

    def arrive(d, piece):
        @pl.when(i >= d)
        def _():
            hop(0, d, piece, pair, z_send).wait_recv()

    every = range(PIECES)
    forward(0, every)
    deep = heads * HD // LOADS
    wo_copies = [
        fetch(
            wo_hbm.at[pl.ds(n * deep, deep)], wo.at[pl.ds(n * deep, deep)], in_sem.at[4 + n]
        )
        for n in range(LOADS)
    ]

    scale = HD ** (-0.5) * math.log2(math.e)

    def project(n, _):
        cols = pl.ds(pl.multiple_of(n * 2 * HD, 2 * HD), 2 * HD)
        both = mm(tok[...], wq[:, cols])
        for k in range(2):
            one = norm_rotate(both[:, k * HD : (k + 1) * HD], qg[...] * scale, cos2[...], sin2[...])
            one = one.astype(BF16)
            at = pl.multiple_of((n * 2 + k) * ct, ct)
            for c in range(chunks):
                q_s[c, pl.ds(at, ct), pl.ds(0, HD)] = one[c * ct : (c + 1) * ct]
        return 0

    def query_part(n, _):
        wq_copy(n).wait()
        project(n, 0)

        @pl.when(n >= 1)
        def _():
            forward(2, [n - 1])

        return 0

    lax.fori_loop(0, q_parts, query_part, 0)
    across = (HD, wide)
    starts_down = jnp.broadcast_to(starts.astype(F32), across).T
    ends_down = jnp.broadcast_to(ends.astype(F32), across).T
    starts_down = jnp.concatenate([starts_down] * (rows // HD), axis=1)
    ends_down = jnp.concatenate([ends_down] * (rows // HD), axis=1)
    key_at = lax.broadcasted_iota(jnp.int32, (wide, rows), 1)
    doc_at = lax.broadcasted_iota(jnp.int32, (wide, rows), 0)

    def key_codes(slots):
        for j in slots:
            vt[j, :, pl.ds(HD, HD)] = jnp.ones((rows, HD), BF16)
            place_of = (key_at + (i - nth(j)) * rows).astype(F32)
            member = (place_of >= starts_down) & (place_of < ends_down)
            held = jnp.where(member, HIDE, jnp.where(doc_at == docs, -HIDE, 0.0))
            kt[j, pl.ds(HD, wide), :] = held.astype(BF16)

    key_codes((0, 1))
    q_code = jnp.where(mine | (lanes == docs), 1.0, 0.0).astype(BF16)
    for c in range(chunks):
        for h in range(heads):
            q_s[c, pl.ds(h * ct, ct), pl.ds(HD, wide)] = q_code[c * ct : (c + 1) * ct]
    for d in range(1, reach + 1):

        @pl.when(i < d)
        def _():
            kv[d] = jnp.zeros(kv.shape[1:], BF16)

    forward(2, every[q_parts - 1 :])

    group = min(8, heads)
    grows = group * ct
    groups = heads // group

    def weights_of(c, at, j):
        weights = jnp.exp2(mm(q_s[c, pl.ds(at, grows), :], kt[j]))
        if j == 0:
            token = lax.broadcasted_iota(jnp.int32, (ct, rows), 0) + c * ct
            seen = lax.broadcasted_iota(jnp.int32, (ct, rows), 1) <= token
            weights = jnp.where(seen[None], weights.reshape(group, ct, rows), 0.0)
            weights = weights.reshape(grows, rows)
        return weights.astype(BF16)

    def weighted(c, at, slots):
        weights = jnp.concatenate([weights_of(c, at, j) for j in slots], axis=1)
        return mm(weights, jnp.concatenate([vt[j] for j in slots], axis=0))

    def place(j, d):
        if d % 2:

            @pl.when(i >= d)
            def _():
                for piece in every:
                    hop(0, d, piece, pair, z_send).wait_recv()

        kt[j, pl.ds(0, HD), :] = kv[d, 0].astype(F32).T.astype(BF16)
        vt[j, :, pl.ds(0, HD)] = kv[d, 1]

    def turn(j):
        if j == 0:
            place(0, 0)
            return

        @pl.when(odd)
        def _():
            place(j, j)

        @pl.when(jnp.logical_not(odd))
        def _():
            place(j, j + 1 if j % 2 else j - 1)

    def attend(slots, between=None):
        for j in slots:
            turn(j)

        def step(n, _):
            c = n // groups
            at = pl.multiple_of((n % groups) * grows, grows)
            new = weighted(c, at, slots)
            if slots[0] == 0:
                acc[c, pl.ds(at, grows), :] = new
            else:
                acc[c, pl.ds(at, grows), :] += new
            if between is not None:
                between(n)
            return 0

        lax.fori_loop(0, chunks * groups, step, 0)

    steps = chunks * groups

    def second_hop(n):
        @pl.when(n < PIECES)
        def _():
            forward(4, [n])

    attend((0, 1), second_hop)
    forward(4, every[steps:])
    key_codes(range(2, reach + 1))
    for j in range(2, reach, 2):
        if j > 2:
            forward(j + 2, every)
        attend((j, j + 1))
    turn(reach)

    for copy in wo_copies:
        copy.wait()

    def some_rows(c):
        return pl.ds(pl.multiple_of(c * ct, ct), ct)

    def pair_copy(c, k):
        return pltpu.make_async_remote_copy(
            src_ref=s1.at[c, k - 1],
            dst_ref=r1.at[c, k - 1],
            send_sem=s1_send.at[c, k],
            recv_sem=s1_recv.at[c, k],
            device_id=(i, partner),
            device_id_type=MESH,
        )

    def chip_copy(c, k):
        return pltpu.make_async_remote_copy(
            src_ref=s2.at[c, k - 1],
            dst_ref=r2.at[k - 1, some_rows(c)],
            send_sem=s2_send.at[c, k - 1],
            recv_sem=s2_recv.at[c, k - 1],
            device_id=(i, (t + 2 * k) % n_tp),
            device_id_type=MESH,
        )

    own_copy = pltpu.make_async_remote_copy(
        src_ref=s1_own,
        dst_ref=r1_own,
        send_sem=s1_send.at[0, 0],
        recv_sem=s1_recv.at[0, 0],
        device_id=(i, partner),
        device_id_type=MESH,
    )
    kept = pltpu.make_async_copy(own.at[0], mine_ref, own_sem.at[0])

    def columns(owner):
        return pl.ds(pl.multiple_of(owner * cw, cw), cw)

    def finish(c):
        def step(n, _):
            at = pl.multiple_of(n * grows, grows)
            total = acc[c, pl.ds(at, grows), :] + weighted(c, at, (reach,))
            done = (total[:, :HD] / total[:, HD:]).astype(BF16)
            for h in range(group):
                cols = pl.ds(pl.multiple_of(n * group * HD + h * HD, HD), HD)
                att[some_rows(c), cols] = done[h * ct : (h + 1) * ct]
            return 0

        if groups == 1:
            step(0, 0)
        else:
            lax.fori_loop(0, groups, step, 0)

    def pair_sum(c):
        for k in range(1, nb):
            pair_copy(c, k).wait_recv()
            term = own[k, some_rows(c)] + r1[c, k - 1].astype(F32)
            s2[c, k - 1] = term.astype(BF16)
            chip_copy(c, k).start()

    def chunk(c, _):
        finish(c)

        @pl.when(c >= 1)
        def _():
            pair_sum(c - 1)

        for k in range(1, nb):
            term = mm(att[some_rows(c)], wo[:, columns((partner + 2 * k) % n_tp)])
            s1[c, k - 1] = term.astype(BF16)
            pair_copy(c, k).start()
        for k in range(1, nb):
            term = mm(att[some_rows(c)], wo[:, columns((t + 2 * k) % n_tp)])
            own[k, some_rows(c)] = term.astype(BF16).astype(F32)
        return 0

    lax.fori_loop(0, chunks, chunk, 0)
    pair_sum(chunks - 1)
    s1_own[...] = mm(att[...], wo[:, columns(partner)]).astype(BF16)
    own_copy.start()
    own[0] = mm(att[...], wo[:, columns(t)]).astype(BF16).astype(F32)
    own_copy.wait_recv()
    own[0] += r1_own[...].astype(F32)
    kept.start()
    own_copy.wait_send()
    kept.wait()
    for c in range(chunks):
        for k in range(1, nb):
            pair_copy(c, k).wait_send()
            chip_copy(c, k).wait_send()
    for d in range(0, reach + 1, 2):
        for piece in every:
            for cond, copy in hops(d, piece):

                @pl.when(cond)
                def _():
                    copy.wait_send()
    for c in range(chunks):
        for k in range(1, nb):
            chip_copy(c, k).wait_recv()


def local(n_ctx, n_tp, tokens, w_query, w_key, w_value, w_out, query_gain, key_gain, doc_lengths):
    rows, width = tokens.shape
    heads = w_query.shape[1] // HD
    out_width = w_out.shape[1]
    reach = min(16, n_ctx // 2)
    docs = doc_lengths.shape[0]
    wide = -(-(docs + 1) // 128) * 128
    chunks = CHUNKS
    ct = rows // chunks
    nb = n_tp // 2
    cw = out_width // n_tp
    dma = pltpu.SemaphoreType.DMA
    anywhere = pl.BlockSpec(memory_space=pltpu.HBM)
    macs = rows * width * (heads + 2) * HD + rows * heads * HD * out_width
    macs += 2 * rows * heads * rows * (reach + 1) * 2 * HD
    mine, others = pl.pallas_call(
        functools.partial(kernel, reach, n_ctx, n_tp, docs),
        out_shape=(
            jax.ShapeDtypeStruct((rows, cw), F32),
            jax.ShapeDtypeStruct((nb - 1, rows, cw), BF16),
        ),
        in_specs=[anywhere] * 9,
        out_specs=(anywhere, anywhere),
        scratch_shapes=[
            pltpu.SMEM((docs,), jnp.int32),
            pltpu.VMEM((rows, width), BF16),
            pltpu.VMEM((width, 2 * HD), BF16),
            pltpu.VMEM((width, heads * HD), BF16),
            pltpu.VMEM((heads * HD, out_width), BF16),
            pltpu.VMEM((1, HD), F32),
            pltpu.VMEM((1, HD), F32),
            pltpu.VMEM((1, HD), F32),
            pltpu.VMEM((rows, HD), F32),
            pltpu.VMEM((rows, HD), F32),
            pltpu.VMEM((reach + 1, 2, rows, HD), BF16),
            pltpu.VMEM((reach + 1, HD + wide, rows), BF16),
            pltpu.VMEM((reach + 1, rows, 2 * HD), BF16),
            pltpu.VMEM((chunks, heads * ct, HD + wide), BF16),
            pltpu.VMEM((chunks, heads * ct, 2 * HD), F32),
            pltpu.VMEM((rows, heads * HD), BF16),
            pltpu.VMEM((chunks, nb - 1, ct, cw), BF16),
            pltpu.VMEM((chunks, nb - 1, ct, cw), BF16),
            pltpu.VMEM((chunks, nb - 1, ct, cw), BF16),
            pltpu.VMEM((rows, cw), BF16),
            pltpu.VMEM((rows, cw), BF16),
            pltpu.VMEM((nb, rows, cw), F32),
            dma((4 + LOADS,)),
            dma((3, LOADS)),
            dma((heads // 2,)),
            dma((chunks,)),
            dma((reach // 2 + 1, PIECES)),
            dma((reach // 2 + 1, PIECES)),
            dma((reach + 1, PIECES)),
            dma((chunks, nb)),
            dma((chunks, nb)),
            dma((chunks, nb - 1)),
            dma((chunks, nb - 1)),
        ],
        compiler_params=pltpu.CompilerParams(
            collective_id=0, has_side_effects=True, vmem_limit_bytes=64 * 2**20
        ),
        cost_estimate=pl.CostEstimate(
            flops=2 * macs,
            bytes_accessed=2 * (tokens.size + w_query.size + w_out.size + 2 * width * HD),
            transcendentals=rows * heads * rows * (reach + 1),
        ),
        name="attention_layer",
    )(
        doc_lengths, tokens, w_query, w_key, w_value, w_out,
        query_gain.reshape(1, HD), key_gain.reshape(1, HD), jnp.asarray(turns_per_token()),
    )
    return (mine + jnp.sum(others.astype(F32), axis=0)).astype(BF16)


def solution(mesh):
    return jax.shard_map(
        functools.partial(local, mesh.shape["ctx"], mesh.shape["tp"]),
        mesh=mesh,
        in_specs=(P("ctx", None), P(None, "tp"), P(), P(), P("tp", None), P(), P(), P()),
        out_specs=P("ctx", "tp"),
        check_vma=False,
    )
```

```python
import functools
import math

import jax
import jax.numpy as jnp
import numpy as np
from jax import lax
from jax.experimental import pallas as pl
from jax.experimental.pallas import tpu as pltpu
from jax.sharding import PartitionSpec as P

H = 32
KVH = 4
HD = 128
EPSILON = 1e-06
ROPE_BASE = 1000000.0
HIDE = 256.0
CHUNKS = 4
PIECES = 4
LOADS = 4
MESH = pl.DeviceIdType.MESH
BF16 = jnp.bfloat16
F32 = jnp.float32


def turns_per_token():
    half = HD // 2
    freq = ROPE_BASE ** (-2.0 * np.arange(half) / HD) / (2 * math.pi)
    return np.concatenate([freq, freq])[None, :].astype(np.float32)


def cos_of_turns(turns):
    x = (turns - jnp.round(turns)) * (2 * math.pi)
    x2 = x * x
    out = jnp.full_like(x2, 1.0 / math.factorial(16))
    for n in range(14, -1, -2):
        out = out * x2 + (-1.0) ** (n // 2) / math.factorial(n)
    return out


def mm(a, b):
    return jnp.dot(a, b, preferred_element_type=F32)


def norm_rotate(u, gain, cos2, sin2):
    inv = lax.rsqrt(jnp.mean(u * u, axis=-1, keepdims=True) + EPSILON)
    w = u * inv * gain
    return w * cos2 + pltpu.roll(w, HD // 2, 1) * sin2


def kernel(
    reach, n_ctx, n_tp, docs,
    docs_hbm, tok_hbm, wq_hbm, wk_hbm, wv_hbm, wo_hbm, qg_hbm, kg_hbm, fr_hbm,
    mine_ref, r2,
    docs_ref, tok, wkv, wq, wo, qg, kg, fr, cos2, sin2, kv, kt, vt, q_s, acc, att, s1, r1, s2, s1_own, r1_own, own,
    in_sem, tok_sem, wq_sem, own_sem, z_send, y_send, kv_recv, s1_send, s1_recv, s2_send, s2_recv,
):
    rows = tok.shape[0]
    heads = wq.shape[1] // HD
    wide = kt.shape[1] - HD
    chunks, qrows, _ = q_s.shape
    ct = rows // chunks
    nb = n_tp // 2
    cw = mine_ref.shape[1]
    i = lax.axis_index("ctx")
    t = lax.axis_index("tp")
    pair = i + 1 - 2 * (i % 2)
    odd = i % 2 == 1
    partner = t + 1 - 2 * (t % 2)
    kv_head = t * heads // (H // KVH)

    def fetch(src, dst, sem):
        copy = pltpu.make_async_copy(src, dst, sem)
        copy.start()
        return copy

    kv_cols = pl.ds(pl.multiple_of(kv_head * HD, HD), HD)
    small = [
        fetch(docs_hbm, docs_ref, in_sem.at[0]),
        fetch(fr_hbm, fr, in_sem.at[1]),
        fetch(qg_hbm, qg, in_sem.at[2]),
        fetch(kg_hbm, kg, in_sem.at[3]),
    ]
    first = []
    for n in range(LOADS):
        some = pl.ds(n * (rows // LOADS), rows // LOADS)
        first.append(fetch(tok_hbm.at[some], tok.at[some], tok_sem.at[0, n]))
        deep = pl.ds(n * (wkv.shape[0] // LOADS), wkv.shape[0] // LOADS)
        first.append(fetch(wk_hbm.at[deep, kv_cols], wkv.at[deep, pl.ds(0, HD)], tok_sem.at[1, n]))
        first.append(fetch(wv_hbm.at[deep, kv_cols], wkv.at[deep, pl.ds(HD, HD)], tok_sem.at[2, n]))
    q_parts = heads // 2

    def wq_copy(n):
        cols = pl.ds(pl.multiple_of(n * 2 * HD, 2 * HD), 2 * HD)
        return pltpu.make_async_copy(wq_hbm.at[:, cols], wq.at[:, cols], wq_sem.at[n])

    barrier = pltpu.get_barrier_semaphore()

    def greet(where):
        pl.semaphore_signal(barrier, inc=1, device_id=where, device_id_type=MESH)

    greet((pair, t))
    greet((i, partner))
    for step in range(1, nb):
        greet((i, (t + 2 * step) % n_tp))

    @pl.when(i >= 2)
    def _():
        greet((i - 2, t))

    @pl.when(i + 2 < n_ctx)
    def _():
        greet((i + 2, t))

    lane = lax.broadcasted_iota(jnp.int32, (1, wide), 1)

    small[0].wait()

    def add_doc(d, state):
        begin, starts, ends = state
        end = begin + docs_ref[d]
        starts = jnp.where(lane == d, begin, starts)
        ends = jnp.where(lane == d, end, ends)
        return end, starts, ends

    nothing = jnp.full((1, wide), -1, jnp.int32)
    _, starts, ends = lax.fori_loop(0, docs, add_doc, (jnp.int32(0), nothing, nothing))
    local = lax.broadcasted_iota(jnp.int32, (rows, wide), 0)
    lanes = lax.broadcasted_iota(jnp.int32, (rows, wide), 1)

    def nth(j):
        if j == 0:
            return 0
        return j + (1 - i % 2) * (1 if j % 2 else -1)

    def members(d):
        pos = local + (i - d) * rows
        return (pos >= starts) & (pos < ends)

    mine = members(0)
    start = jnp.sum(jnp.where(mine, starts, 0).astype(F32), axis=1, keepdims=True)
    pos = (lax.broadcasted_iota(jnp.int32, (rows, HD), 0) + i * rows).astype(F32)
    for copy in small[1:]:
        copy.wait()
    turns = (pos - start) * fr[...]
    low = lax.broadcasted_iota(jnp.int32, (rows, HD), 1) < HD // 2
    cos2[...] = cos_of_turns(turns)
    sine = cos_of_turns(turns - 0.25)
    sin2[...] = jnp.where(low, -sine, sine)

    for n in range(q_parts):
        wq_copy(n).start()
    for copy in first:
        copy.wait()
    projected = mm(tok[...], wkv[...])
    kv[0, 0] = norm_rotate(projected[:, :HD], kg[...], cos2[...], sin2[...]).astype(BF16)
    kv[0, 1] = projected[:, HD:].astype(BF16)

    greeted = 1 + nb + jnp.where(i >= 2, 1, 0) + jnp.where(i + 2 < n_ctx, 1, 0)
    pl.semaphore_wait(barrier, greeted)

    part = rows // PIECES

    def hop(src, dst, piece, where, sems):
        here = (slice(None), pl.ds(pl.multiple_of(piece * part, part), part), slice(None))
        return pltpu.make_async_remote_copy(
            src_ref=kv.at[(src,) + here],
            dst_ref=kv.at[(dst,) + here],
            send_sem=sems.at[src // 2, piece],
            recv_sem=kv_recv.at[dst, piece],
            device_id=(where, t),
            device_id_type=MESH,
        )

    def hops(d, piece):
        there = i >= d
        moves = []
        if d + 2 <= reach:
            moves.append((there & (i + 2 < n_ctx), hop(d, d + 2, piece, i + 2, z_send)))
        if d + 1 <= reach:
            moves.append((there & jnp.logical_not(odd), hop(d, d + 1, piece, pair, y_send)))
        if d >= 2:
            moves.append((there & odd, hop(d, d - 1, piece, pair, y_send)))
        return moves

    def forward(d, pieces):
        for piece in pieces:
            if d:
                arrive(d, piece)
            for cond, copy in hops(d, piece):

                @pl.when(cond)
                def _():
                    copy.start()

    def arrive(d, piece):
        @pl.when(i >= d)
        def _():
            hop(0, d, piece, pair, z_send).wait_recv()

    every = range(PIECES)
    forward(0, every)
    deep = heads * HD // LOADS
    wo_copies = [
        fetch(
            wo_hbm.at[pl.ds(n * deep, deep)], wo.at[pl.ds(n * deep, deep)], in_sem.at[4 + n]
        )
        for n in range(LOADS)
    ]

    scale = HD ** (-0.5) * math.log2(math.e)

    def project(n, _):
        cols = pl.ds(pl.multiple_of(n * 2 * HD, 2 * HD), 2 * HD)
        both = mm(tok[...], wq[:, cols])
        for k in range(2):
            one = norm_rotate(both[:, k * HD : (k + 1) * HD], qg[...] * scale, cos2[...], sin2[...])
            one = one.astype(BF16)
            at = pl.multiple_of((n * 2 + k) * ct, ct)
            for c in range(chunks):
                q_s[c, pl.ds(at, ct), pl.ds(0, HD)] = one[c * ct : (c + 1) * ct]
        return 0

    def query_part(n, _):
        wq_copy(n).wait()
        project(n, 0)

        @pl.when(n >= 1)
        def _():
            forward(2, [n - 1])

        return 0

    lax.fori_loop(0, q_parts, query_part, 0)
    across = (HD, wide)
    starts_down = jnp.broadcast_to(starts.astype(F32), across).T
    ends_down = jnp.broadcast_to(ends.astype(F32), across).T
    starts_down = jnp.concatenate([starts_down] * (rows // HD), axis=1)
    ends_down = jnp.concatenate([ends_down] * (rows // HD), axis=1)
    key_at = lax.broadcasted_iota(jnp.int32, (wide, rows), 1)
    doc_at = lax.broadcasted_iota(jnp.int32, (wide, rows), 0)

    def key_codes(slots):
        for j in slots:
            vt[j, :, pl.ds(HD, HD)] = jnp.ones((rows, HD), BF16)
            place_of = (key_at + (i - nth(j)) * rows).astype(F32)
            member = (place_of >= starts_down) & (place_of < ends_down)
            held = jnp.where(member, HIDE, jnp.where(doc_at == docs, -HIDE, 0.0))
            kt[j, pl.ds(HD, wide), :] = held.astype(BF16)

    key_codes((0, 1))
    q_code = jnp.where(mine | (lanes == docs), 1.0, 0.0).astype(BF16)
    for c in range(chunks):
        for h in range(heads):
            q_s[c, pl.ds(h * ct, ct), pl.ds(HD, wide)] = q_code[c * ct : (c + 1) * ct]
    for d in range(1, reach + 1):

        @pl.when(i < d)
        def _():
            kv[d] = jnp.zeros(kv.shape[1:], BF16)

    forward(2, every[q_parts - 1 :])

    group = min(8, heads)
    grows = group * ct
    groups = heads // group

    def weights_of(c, at, j):
        weights = jnp.exp2(mm(q_s[c, pl.ds(at, grows), :], kt[j]))
        if j == 0:
            token = lax.broadcasted_iota(jnp.int32, (ct, rows), 0) + c * ct
            seen = lax.broadcasted_iota(jnp.int32, (ct, rows), 1) <= token
            weights = jnp.where(seen[None], weights.reshape(group, ct, rows), 0.0)
            weights = weights.reshape(grows, rows)
        return weights.astype(BF16)

    def weighted(c, at, slots):
        weights = jnp.concatenate([weights_of(c, at, j) for j in slots], axis=1)
        return mm(weights, jnp.concatenate([vt[j] for j in slots], axis=0))

    def place(j, d):
        if d % 2:

            @pl.when(i >= d)
            def _():
                for piece in every:
                    hop(0, d, piece, pair, z_send).wait_recv()

        kt[j, pl.ds(0, HD), :] = kv[d, 0].astype(F32).T.astype(BF16)
        vt[j, :, pl.ds(0, HD)] = kv[d, 1]

    def turn(j):
        if j == 0:
            place(0, 0)
            return

        @pl.when(odd)
        def _():
            place(j, j)

        @pl.when(jnp.logical_not(odd))
        def _():
            place(j, j + 1 if j % 2 else j - 1)

    def attend(slots, between=None):
        for j in slots:
            turn(j)

        def step(n, _):
            c = n // groups
            at = pl.multiple_of((n % groups) * grows, grows)
            new = weighted(c, at, slots)
            if slots[0] == 0:
                acc[c, pl.ds(at, grows), :] = new
            else:
                acc[c, pl.ds(at, grows), :] += new
            if between is not None:
                between(n)
            return 0

        lax.fori_loop(0, chunks * groups, step, 0)

    steps = chunks * groups

    def second_hop(n):
        @pl.when(n < PIECES)
        def _():
            forward(4, [n])

    attend((0, 1), second_hop)
    forward(4, every[steps:])
    key_codes(range(2, reach + 1))
    for j in range(2, reach, 2):
        if j > 2:
            forward(j + 2, every)
        attend((j, j + 1))
    turn(reach)

    for copy in wo_copies:
        copy.wait()

    def some_rows(c):
        return pl.ds(pl.multiple_of(c * ct, ct), ct)

    def pair_copy(c, k):
        return pltpu.make_async_remote_copy(
            src_ref=s1.at[c, k - 1],
            dst_ref=r1.at[c, k - 1],
            send_sem=s1_send.at[c, k],
            recv_sem=s1_recv.at[c, k],
            device_id=(i, partner),
            device_id_type=MESH,
        )

    def chip_copy(c, k):
        return pltpu.make_async_remote_copy(
            src_ref=s2.at[c, k - 1],
            dst_ref=r2.at[k - 1, some_rows(c)],
            send_sem=s2_send.at[c, k - 1],
            recv_sem=s2_recv.at[c, k - 1],
            device_id=(i, (t + 2 * k) % n_tp),
            device_id_type=MESH,
        )

    own_copy = pltpu.make_async_remote_copy(
        src_ref=s1_own,
        dst_ref=r1_own,
        send_sem=s1_send.at[0, 0],
        recv_sem=s1_recv.at[0, 0],
        device_id=(i, partner),
        device_id_type=MESH,
    )
    kept = pltpu.make_async_copy(own.at[0], mine_ref, own_sem.at[0])

    def columns(owner):
        return pl.ds(pl.multiple_of(owner * cw, cw), cw)

    def finish(c):
        def step(n, _):
            at = pl.multiple_of(n * grows, grows)
            total = acc[c, pl.ds(at, grows), :] + weighted(c, at, (reach,))
            done = (total[:, :HD] / total[:, HD:]).astype(BF16)
            for h in range(group):
                cols = pl.ds(pl.multiple_of(n * group * HD + h * HD, HD), HD)
                att[some_rows(c), cols] = done[h * ct : (h + 1) * ct]
            return 0

        if groups == 1:
            step(0, 0)
        else:
            lax.fori_loop(0, groups, step, 0)

    def pair_sum(c):
        for k in range(1, nb):
            pair_copy(c, k).wait_recv()
            term = own[k, some_rows(c)] + r1[c, k - 1].astype(F32)
            s2[c, k - 1] = term.astype(BF16)
            chip_copy(c, k).start()

    def chunk(c, _):
        finish(c)

        @pl.when(c >= 1)
        def _():
            pair_sum(c - 1)

        for k in range(1, nb):
            term = mm(att[some_rows(c)], wo[:, columns((partner + 2 * k) % n_tp)])
            s1[c, k - 1] = term.astype(BF16)
            pair_copy(c, k).start()
        for k in range(1, nb):
            term = mm(att[some_rows(c)], wo[:, columns((t + 2 * k) % n_tp)])
            own[k, some_rows(c)] = term.astype(BF16).astype(F32)
        return 0

    lax.fori_loop(0, chunks, chunk, 0)
    pair_sum(chunks - 1)
    s1_own[...] = mm(att[...], wo[:, columns(partner)]).astype(BF16)
    own_copy.start()
    own[0] = mm(att[...], wo[:, columns(t)]).astype(BF16).astype(F32)
    own_copy.wait_recv()
    own[0] += r1_own[...].astype(F32)
    kept.start()
    own_copy.wait_send()
    kept.wait()
    for c in range(chunks):
        for k in range(1, nb):
            pair_copy(c, k).wait_send()
            chip_copy(c, k).wait_send()
    for d in range(0, reach + 1, 2):
        for piece in every:
            for cond, copy in hops(d, piece):

                @pl.when(cond)
                def _():
                    copy.wait_send()
    for c in range(chunks):
        for k in range(1, nb):
            chip_copy(c, k).wait_recv()


def local(n_ctx, n_tp, tokens, w_query, w_key, w_value, w_out, query_gain, key_gain, doc_lengths):
    rows, width = tokens.shape
    heads = w_query.shape[1] // HD
    out_width = w_out.shape[1]
    reach = min(16, n_ctx // 2)
    docs = doc_lengths.shape[0]
    wide = -(-(docs + 1) // 128) * 128
    chunks = CHUNKS
    ct = rows // chunks
    nb = n_tp // 2
    cw = out_width // n_tp
    dma = pltpu.SemaphoreType.DMA
    anywhere = pl.BlockSpec(memory_space=pltpu.HBM)
    macs = rows * width * (heads + 2) * HD + rows * heads * HD * out_width
    macs += 2 * rows * heads * rows * (reach + 1) * 2 * HD
    mine, others = pl.pallas_call(
        functools.partial(kernel, reach, n_ctx, n_tp, docs),
        out_shape=(
            jax.ShapeDtypeStruct((rows, cw), F32),
            jax.ShapeDtypeStruct((nb - 1, rows, cw), BF16),
        ),
        in_specs=[anywhere] * 9,
        out_specs=(anywhere, anywhere),
        scratch_shapes=[
            pltpu.SMEM((docs,), jnp.int32),
            pltpu.VMEM((rows, width), BF16),
            pltpu.VMEM((width, 2 * HD), BF16),
            pltpu.VMEM((width, heads * HD), BF16),
            pltpu.VMEM((heads * HD, out_width), BF16),
            pltpu.VMEM((1, HD), F32),
            pltpu.VMEM((1, HD), F32),
            pltpu.VMEM((1, HD), F32),
            pltpu.VMEM((rows, HD), F32),
            pltpu.VMEM((rows, HD), F32),
            pltpu.VMEM((reach + 1, 2, rows, HD), BF16),
            pltpu.VMEM((reach + 1, HD + wide, rows), BF16),
            pltpu.VMEM((reach + 1, rows, 2 * HD), BF16),
            pltpu.VMEM((chunks, heads * ct, HD + wide), BF16),
            pltpu.VMEM((chunks, heads * ct, 2 * HD), F32),
            pltpu.VMEM((rows, heads * HD), BF16),
            pltpu.VMEM((chunks, nb - 1, ct, cw), BF16),
            pltpu.VMEM((chunks, nb - 1, ct, cw), BF16),
            pltpu.VMEM((chunks, nb - 1, ct, cw), BF16),
            pltpu.VMEM((rows, cw), BF16),
            pltpu.VMEM((rows, cw), BF16),
            pltpu.VMEM((nb, rows, cw), F32),
            dma((4 + LOADS,)),
            dma((3, LOADS)),
            dma((heads // 2,)),
            dma((chunks,)),
            dma((reach // 2 + 1, PIECES)),
            dma((reach // 2 + 1, PIECES)),
            dma((reach + 1, PIECES)),
            dma((chunks, nb)),
            dma((chunks, nb)),
            dma((chunks, nb - 1)),
            dma((chunks, nb - 1)),
        ],
        compiler_params=pltpu.CompilerParams(
            collective_id=0, has_side_effects=True, vmem_limit_bytes=64 * 2**20
        ),
        cost_estimate=pl.CostEstimate(
            flops=2 * macs,
            bytes_accessed=2 * (tokens.size + w_query.size + w_out.size + 2 * width * HD),
            transcendentals=rows * heads * rows * (reach + 1),
        ),
        name="attention_layer",
    )(
        doc_lengths, tokens, w_query, w_key, w_value, w_out,
        query_gain.reshape(1, HD), key_gain.reshape(1, HD), jnp.asarray(turns_per_token()),
    )
    return (mine + jnp.sum(others.astype(F32), axis=0)).astype(BF16)


def solution(mesh):
    return jax.shard_map(
        functools.partial(local, mesh.shape["ctx"], mesh.shape["tp"]),
        mesh=mesh,
        in_specs=(P("ctx", None), P(None, "tp"), P(), P(), P("tp", None), P(), P(), P()),
        out_specs=P("ctx", "tp"),
        check_vma=False,
    )
```
